256 devices in a mesh: dp: 32 (over z, x), hst: 8 (over y, core).
Axes of the slice: x: 4, y: 4, z: 8, core: 2. Of those that a mesh axis runs over, the one named last changes fastest.
Arguments:
- tokens: bfloat16 [512, 7168], P('dp', 'hst'), may hold values from -6 to 6
- cotangent: bfloat16 [512, 7168], P('dp', 'hst'), may hold values from -6 to 6
- expert_ids: int32 [512, 2], P('dp'), may hold values from 0 to 7, all different within a row; in each aligned block of 16 rows (0 to 15, 16 to 31, ...) at most 4 rows name the same one
- gate_values: float32 [512, 2], P('dp'), may hold values from 0.2 to 1
- w_gate: bfloat16 [8, 4864, 7168], P('hst', 'dp'), may hold values from -0.0625 to 0.0625
- w_up: bfloat16 [8, 4864, 7168], P('hst', 'dp'), may hold values from -0.0625 to 0.0625
- w_down: bfloat16 [8, 4864, 7168], P('hst', 'dp'), may hold values from -0.078125 to 0.078125
Outputs:
- mixed: bfloat16 [512, 7168], P('dp', 'hst')
- grad_tokens: bfloat16 [512, 7168], P('dp', 'hst')
- grad_gate: bfloat16 [8, 4864, 7168], P('hst', 'dp')
- grad_up: bfloat16 [8, 4864, 7168], P('hst', 'dp')
- grad_down: bfloat16 [8, 4864, 7168], P('hst', 'dp')
The draws below stay inside these ranges and needn't reach their ends.
Inputs may be any that keep to these rules, and one draw needn't show every extreme that they name: `expert_ids`: within each block of 16 rows (the rows of one index of dp), a token names two different experts, and no expert is named by more than 4 routes; since a block has 32 routes and 32 slots, every expert fills all 4 of its slots in every block.
All inputs are finite; a program needn't handle non-finite values.
Results may differ from the reference program's by a relative error of at most 0.023.
Values may be sent and summed in bfloat16 or wider, within the bound.
A program may use at most 128 MiB of HBM per device.

```python
import math
import jax
import jax.numpy as jnp
import numpy as np
from jax import lax

D = 7168
FF_E = 4864
EXPERTS = 8
TOK_DEV = 16
CAP = 4
TOKENS = 512
N_DP = 32


def levels(rng, dims, cuts, least, largest):
    factor_of, own = 1.0, jax.random.fold_in(rng, 6)
    for dim, shards_of in cuts:
        heights = jnp.exp(jax.random.uniform(jax.random.fold_in(own, dim), (shards_of,), jnp.float32, least / len(cuts), largest / len(cuts)))
        factor_of = factor_of * jnp.repeat(heights, dims[dim] // shards_of).reshape([-1 if axis == dim else 1 for axis in range(len(dims))])
    return factor_of


def assign_block(rng, own, number, rows, number_of, top, reach, skew):
    sequence = jax.random.permutation(rng, number_of)
    packed, common = portions_of(number_of, rows * top, reach, skew, True), portions_of(number_of, rows * top, reach, skew, False)
    places = jnp.arange(number_of)

    def named(sizes, rotation):
        used = int((sizes > 0).sum())
        fixed = max(1, used // 4)
        passed = fixed + (places - fixed + rotation * (used - fixed)) % max(1, number_of - fixed)
        return jnp.zeros((number_of,), jnp.int32).at[sequence[jnp.where(places < fixed, places, passed)]].set(jnp.asarray(sizes, jnp.int32))

    sizes = jnp.where(number % 4 == 0, named(packed, number // 4), named(common, number - number // 4 - 1))
    mixed = jax.random.permutation(jax.random.fold_in(own, 3), number_of)
    donor, sink = mixed[0:number_of // 2 * 2:2], mixed[1:number_of // 2 * 2:2]
    slack = jnp.minimum(sizes[donor] - 1, reach - sizes[sink]) // 2
    slack = jnp.where((donor == sequence[0]) | (sink == sequence[0]) | (sizes[sink] == 0), 0, jnp.maximum(slack, 0))
    passed = jax.random.randint(jax.random.fold_in(own, 4), (number_of // 2,), 0, 1 << 20) % (slack + 1)
    sizes = sizes.at[donor].add(-passed).at[sink].add(passed)
    items = jnp.searchsorted(jnp.cumsum(sizes), jnp.arange(rows * top), side="right").astype(jnp.int32)
    grid = items.reshape(top, rows).T
    grid = grid[jax.random.permutation(jax.random.fold_in(own, 1), rows)]
    rotation = jax.random.randint(jax.random.fold_in(own, 2), (rows, 1), 0, top)
    return jnp.take_along_axis(grid, (jnp.arange(top)[None, :] + rotation) % top, axis=1)


def portions_of(number_of, total, limit, skew, full):
    loads = [(1 << 20) // math.isqrt(grade ** skew) + 1 for grade in range(1, number_of + 1)]
    largest = limit if full else min(limit, max(-(-total // number_of), total * loads[0] // sum(loads)))
    least = 1 if total - largest >= number_of - 1 else 0
    given, rest = [largest] + [least] * (number_of - 1), total - largest - least * (number_of - 1)
    while rest > 0:
        candidates = [i for i in range(1, number_of) if given[i] < largest] or [i for i in range(1, number_of) if given[i] < limit]
        pool, left = sum([loads[i] for i in candidates]), rest
        for i in candidates:
            addition = min(limit - given[i], max(1, left * loads[i] // pool), rest)
            given[i] = given[i] + addition
            rest = rest - addition
    return np.array(given)


def noise(key, shape, scale, reach, cuts=(), kind=jnp.bfloat16):
    result = jax.random.normal(key, shape, jnp.float32) * scale
    if len(cuts) > 0:
        result = levels(key, shape, cuts, -0.22, 0.18) * result
    return jnp.clip(result, min=-reach, max=reach).astype(kind)


def setup_inputs(seed: int = 0) -> dict:
    streams_of = jax.random.split(jax.random.key(seed), 8)
    tokens = noise(streams_of[0], (TOKENS, D), 1.0, 6.0, ((0, 32), (1, 8)))
    cotangent = noise(streams_of[1], (TOKENS, D), 1.0, 6.0, ((0, 32), (1, 8)))
    expert_ids_keys = jax.random.split(jax.random.fold_in(streams_of[2], 1), TOKENS // TOK_DEV)
    expert_ids_turns = jax.random.permutation(jax.random.fold_in(streams_of[2], 3), TOKENS // TOK_DEV)
    expert_ids = jax.vmap(lambda own, number: assign_block(jax.random.fold_in(streams_of[2], 2), own, number, TOK_DEV, EXPERTS, 2, CAP, 1))(expert_ids_keys, expert_ids_turns).reshape((TOKENS, 2))
    gate_values = jnp.clip(0.2 + 0.8 * jax.random.uniform(streams_of[3], (TOKENS, 2), jnp.float32) ** levels(streams_of[3], (TOKENS, 2), ((0, 32),), -0.2, 0.2), 0.2, 1.0)
    w_gate = noise(streams_of[4], (EXPERTS, FF_E, D), D ** -0.5, 0.0625, ((0, 8), (1, 32)))
    w_up = noise(streams_of[5], (EXPERTS, FF_E, D), D ** -0.5, 0.0625, ((0, 8), (1, 32)))
    w_down = noise(streams_of[6], (EXPERTS, FF_E, D), FF_E ** -0.5, 0.078125, ((0, 8), (1, 32)))
    return dict(tokens=tokens, cotangent=cotangent, expert_ids=expert_ids, gate_values=gate_values, w_gate=w_gate, w_up=w_up, w_down=w_down)


def route_tables(expert_ids, gate_values, experts, cap):
    count = expert_ids.shape[0]
    flat = expert_ids.reshape(-1)
    labels = jnp.arange(experts, dtype=jnp.int32)
    onehot = (flat[:, None] == labels[None, :]).astype(jnp.int32)
    position = jnp.cumsum(onehot, axis=0) - onehot
    slot = jnp.sum(position * onehot, axis=1)
    slots = jnp.arange(cap, dtype=jnp.int32)
    hit = (flat[:, None, None] == labels[None, :, None]) & (slot[:, None, None] == slots[None, None, :])
    hit = hit.astype(jnp.float32).reshape(count, 2, experts, cap)
    select = jnp.transpose(jnp.sum(hit, axis=1), (1, 2, 0))
    weigh = jnp.transpose(jnp.sum(hit * gate_values[:, :, None, None], axis=1), (1, 2, 0))
    return select, weigh


def sliced_sum(left, right, width, pieces, rows):
    def add_slice(index, total):
        part = jnp.dot(lax.dynamic_slice_in_dim(left, index * width, width, 1),
                       lax.dynamic_slice_in_dim(right, index * width, width, 0),
                       preferred_element_type=jnp.float32)
        rounded = lax.optimization_barrier(part.astype(jnp.bfloat16))
        return total + rounded.astype(jnp.float32)
    return lax.fori_loop(0, pieces, add_slice, jnp.zeros((rows, right.shape[1]), jnp.float32))


def reference(tokens, cotangent, expert_ids, gate_values, w_gate, w_up, w_down):
    hp = lax.Precision.HIGHEST
    blocks = N_DP
    rows = blocks * CAP
    width = FF_E // N_DP
    x_blocks = tokens.reshape(blocks, TOK_DEV, D).astype(jnp.float32)
    d_blocks = cotangent.reshape(blocks, TOK_DEV, D).astype(jnp.float32)
    select, weigh = jax.vmap(lambda a, b: route_tables(a, b, EXPERTS, CAP))(
        expert_ids.reshape(blocks, TOK_DEV, 2), gate_values.reshape(blocks, TOK_DEV, 2))
    x_rows = jnp.einsum('becT,bTd->ebcd', select, x_blocks, precision=hp).astype(jnp.bfloat16).reshape(EXPERTS, rows, D)
    d_rows = jnp.einsum('becT,bTd->ebcd', weigh, d_blocks, precision=hp).astype(jnp.bfloat16).reshape(EXPERTS, rows, D)

    def one_expert(pack):
        xr, dr, wg, wu, wd = pack
        g = jnp.dot(xr, wg.T, preferred_element_type=jnp.float32)
        u = jnp.dot(xr, wu.T, preferred_element_type=jnp.float32)
        sig = jax.nn.sigmoid(g)
        act = (g * sig * u).astype(jnp.bfloat16)
        out = sliced_sum(act, wd, width, N_DP, rows)
        da = jnp.dot(dr, wd.T, preferred_element_type=jnp.float32)
        dg = (da * u * sig * (1.0 + g * (1.0 - sig))).astype(jnp.bfloat16)
        du = (da * g * sig).astype(jnp.bfloat16)
        gdown = jnp.dot(act.T, dr, preferred_element_type=jnp.float32).astype(jnp.bfloat16)
        ggate = jnp.dot(dg.T, xr, preferred_element_type=jnp.float32).astype(jnp.bfloat16)
        gup = jnp.dot(du.T, xr, preferred_element_type=jnp.float32).astype(jnp.bfloat16)

        def add_slice(index, total):
            dgs = lax.dynamic_slice_in_dim(dg, index * width, width, 1)
            dus = lax.dynamic_slice_in_dim(du, index * width, width, 1)
            wgs = lax.dynamic_slice_in_dim(wg, index * width, width, 0)
            wus = lax.dynamic_slice_in_dim(wu, index * width, width, 0)
            part = jnp.dot(dgs, wgs, preferred_element_type=jnp.float32) + jnp.dot(dus, wus, preferred_element_type=jnp.float32)
            rounded = lax.optimization_barrier(part.astype(jnp.bfloat16))
            return total + rounded.astype(jnp.float32)
        back = lax.fori_loop(0, N_DP, add_slice, jnp.zeros((rows, D), jnp.float32))
        return out, back, ggate, gup, gdown

    outs, backs, grad_gate, grad_up, grad_down = lax.map(one_expert, (x_rows, d_rows, w_gate, w_up, w_down))
    outs = outs.reshape(EXPERTS, blocks, CAP, D)
    backs = backs.reshape(EXPERTS, blocks, CAP, D)
    mixed = jnp.einsum('becT,ebcd->bTd', weigh, outs, precision=hp).astype(jnp.bfloat16).reshape(TOKENS, D)
    grad_tokens = jnp.einsum('becT,ebcd->bTd', select, backs, precision=hp).astype(jnp.bfloat16).reshape(TOKENS, D)
    return mixed, grad_tokens, grad_gate, grad_up, grad_down
```

```python
import jax
import jax.numpy as jnp
from jax import lax
from jax.experimental import pallas as pl
from jax.experimental.pallas import tpu as pltpu
from jax.sharding import PartitionSpec as P

F32, BF16 = jnp.float32, jnp.bfloat16
HIGHEST = lax.Precision.HIGHEST
MESH = pl.DeviceIdType.MESH
NX, NZ, HOSTS, CAP, TOK = 4, 8, 8, 4, 16
ROWS = NX * CAP
R = NZ * ROWS
FEAT = 896
QL = 2 * FEAT
D = NX * QL
FF = 152
LA = 768
TILES = FEAT // 128
MSGS = 192
PLACE = {0: 0, 1: 1, 7: 2, 2: 3, 6: 4, 3: 5, 5: 6, 4: 7}
CHUNKS = ((0, 16), (16, 32), (48, 32), (80, 48))


def rows(k):
    return pl.ds(ROWS * PLACE[k % NZ], ROWS)


def iota(shape, dim):
    return lax.broadcasted_iota(jnp.int32, shape, dim)


def mm(a, b, ca, cb, precision=None):
    return lax.dot_general(
        a, b, (((ca,), (cb,)), ((), ())), precision=precision, preferred_element_type=F32
    )


def add(total, part):
    total[...] = (total[...].astype(F32) + part[...].astype(F32)).astype(BF16)


class Links:
    def __init__(self, ssem, rsem):
        self.ssem, self.rsem, self.sent = ssem, rsem, []

    def send(self, src, dst, land, dev):
        i = len(self.sent)
        copy = pltpu.make_async_remote_copy(
            src_ref=src, dst_ref=dst, send_sem=self.ssem.at[i], recv_sem=self.rsem.at[i],
            device_id=dev, device_id_type=MESH,
        )
        copy.start()
        self.sent.append(copy)
        return pltpu.make_async_remote_copy(
            src_ref=land, dst_ref=land, send_sem=self.ssem.at[i], recv_sem=self.rsem.at[i],
            device_id=dev, device_id_type=MESH,
        ).wait_recv


def ring_steps(*gens):
    for g in gens:
        next(g, None)


def gather(G, links, place):
    x, xp, xm, xo, dxp, dxm, dzp, dzm = place

    def along_x(rs, lo, hi):
        mid = (lo + hi) // 2
        a, b = pl.ds(lo, mid - lo), pl.ds(mid, hi - mid)
        full = pl.ds(lo, hi - lo)
        mine = G.at[x, rs, full]
        p = links.send(mine, mine, G.at[xm, rs, full], dxp)
        m = links.send(mine, mine, G.at[xp, rs, full], dxm)
        yield
        p()
        f = links.send(G.at[xm, rs, a], G.at[xm, rs, a], G.at[xo, rs, a], dxp)
        m()
        g = links.send(G.at[xp, rs, b], G.at[xp, rs, b], G.at[xo, rs, b], dxm)
        yield
        f()
        g()

    def along_z(q, lo, hi):
        mid = (lo + hi) // 2
        p = m = None
        for s in range(1, NZ // 2 + 1):
            if s > 1:
                p()
            lu = pl.ds(lo, hi - lo) if s < NZ // 2 else pl.ds(lo, mid - lo)
            ld = pl.ds(lo, hi - lo) if s < NZ // 2 else pl.ds(mid, hi - mid)
            there = G.at[q, rows(-s), lu]
            p = links.send(G.at[q, rows(1 - s), lu], there, there, dzp)
            if s > 1:
                m()
            there = G.at[q, rows(s), ld]
            m = links.send(G.at[q, rows(s - 1), ld], there, there, dzm)
            yield
        p()
        m()

    a1 = along_x(rows(0), 0, LA)
    b1 = along_z(x, LA, QL)
    b2 = [along_x(pl.ds(lo, n), LA, QL) for lo, n in CHUNKS]
    a2 = [along_z(pl.ds(2 * i, 2), 0, LA) for i in range(2)]
    ring_steps(a1, b1, b2[0])
    yield
    ring_steps(a1, b1, b2[1])
    yield
    ring_steps(a1, a2[0], a2[1])
    yield
    ring_steps(b2[0], b1, b2[2])
    yield
    ring_steps(a2[0], a2[1])
    yield
    ring_steps(b2[1], b1)
    yield
    ring_steps(a2[0], a2[1])
    yield
    ring_steps(b1, b2[3], b2[2])
    yield
    ring_steps(a2[0], a2[1])
    yield
    ring_steps(b2[3])
    yield
    ring_steps(*b2, *a2)


def scatter(O, landing, links, place):
    x, xp, xm, xo, dxp, dxm, dzp, dzm = place
    za, zb, xa1, xa2, xb1, xb2 = landing

    def along_x(rs, lrs, lo, hi, half, whole):
        mid = (lo + hi) // 2
        n = mid - lo
        a, b = pl.ds(lo, n), pl.ds(mid, n)
        full = pl.ds(lo, hi - lo)
        ha, hb = half.at[0, lrs], half.at[1, lrs]
        wa, wb = whole.at[0, lrs], whole.at[1, lrs]
        p = links.send(O.at[xo, rs, a], ha, ha, dxp)
        m = links.send(O.at[xo, rs, b], hb, hb, dxm)
        yield
        p()
        add(O.at[xp, rs, a], ha)
        p = links.send(O.at[xp, rs, full], wa, wa, dxp)
        m()
        add(O.at[xm, rs, b], hb)
        m = links.send(O.at[xm, rs, full], wb, wb, dxm)
        yield
        p()
        add(O.at[x, rs, full], wa)
        m()
        add(O.at[x, rs, full], wb)

    def along_z(q, lq, lo, hi, land):
        mid = (lo + hi) // 2
        n = mid - lo
        a, b = pl.ds(lo, n), pl.ds(mid, n)
        full = pl.ds(lo, hi - lo)

        def at(d, s):
            ref = land.at[d, s] if lq is None else land.at[d, s, lq]
            if s:
                return ref
            return ref.at[:, pl.ds(0, n)] if lq is None else ref.at[:, :, pl.ds(0, n)]

        far = NZ // 2
        m = links.send(O.at[q, rows(far), a], at(0, 0), at(0, 0), dzm)
        p = links.send(O.at[q, rows(far), b], at(1, 0), at(1, 0), dzp)
        yield
        for s in range(1, far):
            k = far - s
            m()
            add(O.at[q, rows(-k), a if s == 1 else full], at(0, s - 1))
            m = links.send(O.at[q, rows(-k), full], at(0, s), at(0, s), dzm)
            p()
            add(O.at[q, rows(k), b if s == 1 else full], at(1, s - 1))
            p = links.send(O.at[q, rows(k), full], at(1, s), at(1, s), dzp)
            yield
        m()
        add(O.at[q, rows(0), full], at(0, far - 1))
        p()
        add(O.at[q, rows(0), full], at(1, far - 1))

    az = [along_z(pl.ds(2 * i, 2), pl.ds(2 * i, 2), 0, LA, za) for i in range(2)]
    bx = [along_x(pl.ds(lo, n), pl.ds(lo, n), LA, QL, xb1, xb2) for lo, n in CHUNKS]
    bz = along_z(x, None, LA, QL, zb)
    ax = along_x(rows(0), slice(None), 0, LA, xa1, xa2)
    ring_steps(*az, bx[3], bx[2])
    yield
    ring_steps(bx[3], bx[1])
    yield
    ring_steps(*az, bx[2], bx[0])
    yield
    ring_steps(bx[3], bz, bx[1])
    yield
    ring_steps(*az)
    yield
    ring_steps(bx[2], bz, bx[0])
    yield
    ring_steps(*az)
    yield
    ring_steps(bx[1], bz)
    yield
    ring_steps(*az, ax)
    yield
    ring_steps(bz, ax, bx[0])
    yield
    ring_steps(bz, ax)


def kernel(
    tok_ref, cot_ref, ids_ref, gate_ref, wg_hbm, wu_hbm, wd_hbm,
    mixed_ref, gtok_ref, gg_hbm, gu_hbm, gd_hbm,
    wg, wu, wd, gx, gd, oo, ob, accg, accu, accd, act_s, dg_s, du_s, grad, qt, qw,
    msend, mrecv, rsend, rrecv, *rest,
):
    land_o, land_b = rest[0:6], rest[6:12]
    wsem, gsem, ssem, rsem, asend, arecv = rest[12:]
    dp, h = lax.axis_index("dp"), lax.axis_index("hst")
    z, x = dp // NX, dp % NX
    xp, xm, xo = (x + 1) % NX, (x + NX - 1) % NX, (x + 2) % NX
    dev = lambda zz, xx, hh: (zz * NX + xx, hh)
    dxp, dxm = dev(z, xp, h), dev(z, xm, h)
    dzp, dzm = dev((z + 1) % NZ, x, h), dev((z + NZ - 1) % NZ, x, h)
    place = (x, xp, xm, xo, dxp, dxm, dzp, dzm)
    hq, hr = h // 2, h % 2
    other = x != hq

    loads = [
        pltpu.make_async_copy(src.at[0], dst, wsem.at[i])
        for i, (src, dst) in enumerate(((wg_hbm, wg), (wu_hbm, wu), (wd_hbm, wd)))
    ]
    for load in loads:
        load.start()

    barrier = pltpu.get_barrier_semaphore()

    def greet(device):
        pl.semaphore_signal(barrier, inc=1, device_id=device, device_id_type=MESH)

    turn = (hq - x + NX) % NX
    greet(dzp)
    greet(dzm)
    for k in range(1, HOSTS):
        greet(dev(z, hq, (h + k) % HOSTS))
    for i in range(1, NX):
        for r in range(2):
            greet(dev(z, (hq + i) % NX, 2 * x + r))

    @pl.when(other)
    def _():
        greet(dev(z, hq, h))

        @pl.when(hq != xp)
        def _():
            greet(dxp)

        @pl.when(hq != xm)
        def _():
            greet(dxm)

    ids, gates = ids_ref[...], gate_ref[...]
    lane = iota((TOK, HOSTS * CAP), 1)
    expert, slot = lane // CAP, (lane % CAP).astype(F32)
    hit0 = (ids[:, 0:1] == expert).astype(F32)
    hit1 = (ids[:, 1:2] == expert).astype(F32)
    below = (iota((TOK, TOK), 0) > iota((TOK, TOK), 1)).astype(BF16)
    before = mm(below, (hit0 + hit1).astype(BF16), 1, 0)
    hit0 = jnp.where(before == slot, hit0, 0.0)
    hit1 = jnp.where(before + (ids[:, 0:1] == expert).astype(F32) == slot, hit1, 0.0)
    wide = (HOSTS * CAP, HOSTS * 32)
    spread = (
        (iota(wide, 0) // CAP == iota(wide, 1) // 32)
        & (iota(wide, 0) % CAP == iota(wide, 1) % CAP)
    ).astype(F32)
    sel = mm(hit0 + hit1, spread, 1, 0, HIGHEST)
    wei = mm(hit0 * gates[:, 0:1] + hit1 * gates[:, 1:2], spread, 1, 0, HIGHEST)
    big = (8 * TOK, HOSTS * 32)
    tile = iota(big, 0) // TOK
    same = (tile == (iota(big, 1) // CAP) % 8) & (tile < TILES)
    qt[...] = jnp.where(same, jnp.concatenate([sel] * 8, axis=0), 0.0)
    qw[...] = jnp.where(same, jnp.concatenate([wei] * 8, axis=0), 0.0)

    def stacked(ref):
        parts = [ref[:, 128 * j : 128 * j + 128] for j in range(TILES)]
        return jnp.concatenate(parts + [jnp.zeros((TOK, 128), ref.dtype)], axis=0)

    xm_rows = mm(qt[...].astype(BF16), stacked(tok_ref), 0, 0).astype(BF16)
    msend[0] = xm_rows.reshape(HOSTS, 32, 128)
    dm_rows = mm(qw[...], stacked(cot_ref).astype(F32), 0, 0, HIGHEST).astype(BF16)
    msend[1] = dm_rows.reshape(HOSTS, 32, 128)

    sq = (128, 128)
    bi, mi = iota(sq, 0), iota(sq, 1)

    def matches(blk, msg):
        return (
            (blk // 16 == (msg // 4) % 8)
            & ((blk // 4) % 4 == msg // 32)
            & (blk % 4 == msg % 4)
        ).astype(F32).astype(BF16)

    into_block, into_msg = matches(bi, mi), matches(mi, bi)

    pl.semaphore_wait(barrier, 18 - 3 * ((NX - turn) // NX) - turn % 2)

    def exchange_out(which):
        copies = []
        for k in range(HOSTS):
            e = (h + k) % HOSTS
            copy = pltpu.make_async_remote_copy(
                src_ref=msend.at[which, e], dst_ref=mrecv.at[which, hr, x],
                send_sem=asend.at[which, k], recv_sem=arecv.at[which, hr * NX + x],
                device_id=dev(z, hq, e), device_id_type=MESH,
            )
            if k:
                copy.start()
            else:
                pl.when(other)(copy.start)
            copies.append(copy)

        @pl.when(jnp.logical_not(other))
        def _():
            mrecv[which, hr, x] = msend[which, h]

        return copies

    def exchange_in(which, block):
        for i in range(NX):
            for r in range(2):
                xi = (x + i) % NX
                land = mrecv.at[which, r, xi]
                copy = pltpu.make_async_remote_copy(
                    src_ref=land, dst_ref=land,
                    send_sem=asend.at[which, 0], recv_sem=arecv.at[which, r * NX + xi],
                    device_id=dev(z, xi, 2 * x + r), device_id_type=MESH,
                )
                if i:
                    copy.wait_recv()
                else:
                    pl.when(2 * x + r != h)(copy.wait_recv)
        for r in range(2):
            got = mm(into_block, mrecv[which, r].reshape(128, 128), 1, 0).astype(BF16)
            for j in range(TILES):
                lo = r * FEAT + 128 * j
                block[x, 0:ROWS, lo : lo + 128] = got[16 * j : 16 * j + 16]

    def return_out(which, block):
        copies = []
        for r in range(2):
            parts = [
                block[x, 0:ROWS, r * FEAT + 128 * j : r * FEAT + 128 * j + 128]
                for j in range(TILES)
            ]
            parts.append(jnp.zeros((ROWS, 128), BF16))
            got = mm(into_msg, jnp.concatenate(parts, axis=0), 1, 0).astype(BF16)
            rsend[which, r] = got.reshape(NX, 32, 128)
        for i in range(NX):
            for r in range(2):
                xi = (x + i) % NX
                copy = pltpu.make_async_remote_copy(
                    src_ref=rsend.at[which, r, xi], dst_ref=rrecv.at[which, h],
                    send_sem=asend.at[2 + which, 2 * i + r], recv_sem=arecv.at[2 + which, h],
                    device_id=dev(z, xi, 2 * x + r), device_id_type=MESH,
                )
                if i:
                    copy.start()
                else:
                    pl.when(2 * x + r != h)(copy.start)
                copies.append(copy)

        @pl.when(jnp.logical_not(other))
        def _():
            rrecv[which, h] = rsend[which, hr, x]

        return copies

    def return_in(which, table, out):
        for k in range(HOSTS):
            e = (h + k) % HOSTS
            land = rrecv.at[which, e]
            copy = pltpu.make_async_remote_copy(
                src_ref=land, dst_ref=land,
                send_sem=asend.at[2 + which, 0], recv_sem=arecv.at[2 + which, e],
                device_id=dev(z, hq, e), device_id_type=MESH,
            )
            if k:
                copy.wait_recv()
            else:
                pl.when(other)(copy.wait_recv)
        got = rrecv[which].reshape(HOSTS * 32, 128).astype(F32)
        res = mm(table[...], got, 1, 0, HIGHEST).astype(BF16)
        for j in range(TILES):
            out[:, 128 * j : 128 * j + 128] = res[16 * j : 16 * j + 16]

    links = Links(ssem, rsem)
    quarter = lambda q: slice(q * QL, (q + 1) * QL)

    def gate_task(q):
        g = mm(gx[q], wg[:, quarter(q)], 1, 1)
        u = mm(gx[q], wu[:, quarter(q)], 1, 1)
        accg[...] = g if q == 0 else accg[...] + g
        accu[...] = u if q == 0 else accu[...] + u

    def act_task():
        g = accg[...]
        act_s[...] = (g * jax.nn.sigmoid(g) * accu[...]).astype(BF16)

    def out_task(q):
        oo[q] = mm(act_s[...], wd[:, quarter(q)], 1, 0).astype(BF16)

    def da_task(q):
        a = mm(gd[q], wd[:, quarter(q)], 1, 1)
        accd[...] = a if q == 0 else accd[...] + a

    def hidden_task():
        g, u, a = accg[...], accu[...], accd[...]
        s = jax.nn.sigmoid(g)
        dg_s[...] = (a * u * s * (1.0 + g * (1.0 - s))).astype(BF16)
        du_s[...] = (a * g * s).astype(BF16)

    def back_task(q):
        part = mm(dg_s[...], wg[:, quarter(q)], 1, 0) + mm(du_s[...], wu[:, quarter(q)], 1, 0)
        ob[q] = part.astype(BF16)

    stores = []

    def grad_task(i, q):
        left, right, out = ((dg_s, gx, gg_hbm), (du_s, gx, gu_hbm), (act_s, gd, gd_hbm))[i]
        grad[i, :, quarter(q)] = mm(left[...], right[q], 0, 0).astype(BF16)
        if q == NX - 1:
            store = pltpu.make_async_copy(grad.at[i], out.at[0], gsem.at[i])
            store.start()
            stores.append(store)

    def task(f, *args):
        return lambda: f(*args)

    def drive(gen, tasks, per=1):
        tasks = list(tasks)
        for _ in gen:
            for t in tasks[:per]:
                t()
            tasks = tasks[per:]
        for t in tasks:
            t()

    quarters = range(NX)
    pending = exchange_out(0) + exchange_out(1)
    exchange_in(0, gx)
    run = gather(gx, links, place)
    next(run)
    exchange_in(1, gd)
    run_d = gather(gd, links, place)
    for step, _ in enumerate(run):
        if step == 8:
            next(run_d)
    loads[0].wait()
    loads[1].wait()
    loads[2].wait()
    tasks = [task(gate_task, q) for q in quarters] + [act_task]
    tasks += [task(out_task, q) for q in quarters]
    drive(run_d, tasks)
    run = scatter(oo, land_o, links, place)
    tasks = [task(da_task, q) for q in quarters] + [hidden_task]
    tasks += [task(back_task, q) for q in quarters]
    drive(run, tasks)
    run = scatter(ob, land_b, links, place)
    next(run)
    pending += return_out(0, oo)
    tasks = [task(grad_task, i, q) for i in range(3) for q in quarters]
    drive(run, tasks, 2)
    pending += return_out(1, ob)
    return_in(0, qw, mixed_ref)
    return_in(1, qt, gtok_ref)

    for store in stores:
        store.wait()
    for copy in links.sent:
        copy.wait_send()
    for n, copy in enumerate(pending):
        first = n < 2 * HOSTS
        if first and n % HOSTS == 0:
            pl.when(other)(copy.wait_send)
        elif not first and n % HOSTS < 2:
            pl.when(2 * x + n % HOSTS != h)(copy.wait_send)
        else:
            copy.wait_send()


def body(tokens, cotangent, expert_ids, gate_values, w_gate, w_up, w_down):
    vmem, hbm = pl.BlockSpec(memory_space=pltpu.VMEM), pl.BlockSpec(memory_space=pl.ANY)
    rows_out = jax.ShapeDtypeStruct((TOK, FEAT), BF16)
    grad_out = jax.ShapeDtypeStruct((1, FF, D), BF16)
    landing = [
        pltpu.VMEM((2, 4, NX, ROWS, LA), BF16),
        pltpu.VMEM((2, 4, ROWS, QL - LA), BF16),
        pltpu.VMEM((2, ROWS, LA // 2), BF16),
        pltpu.VMEM((2, ROWS, LA), BF16),
        pltpu.VMEM((2, R, (QL - LA) // 2), BF16),
        pltpu.VMEM((2, R, QL - LA), BF16),
    ]
    weight, table = pltpu.VMEM((FF, D), BF16), pltpu.VMEM((NX, R, QL), BF16)
    acc, hid = pltpu.VMEM((R, FF), F32), pltpu.VMEM((R, FF), BF16)
    message = pltpu.VMEM((2, HOSTS, 32, 128), BF16)
    blocks = pltpu.VMEM((2, 2, NX, 32, 128), BF16)
    return pl.pallas_call(
        kernel,
        out_shape=(rows_out, rows_out, grad_out, grad_out, grad_out),
        in_specs=[vmem] * 4 + [hbm] * 3,
        out_specs=(vmem, vmem, hbm, hbm, hbm),
        scratch_shapes=[
            weight, weight, weight, table, table, table, table, acc, acc, acc, hid, hid, hid,
            pltpu.VMEM((3, FF, D), BF16),
            pltpu.VMEM((8 * TOK, HOSTS * 32), F32), pltpu.VMEM((8 * TOK, HOSTS * 32), F32),
            message, blocks, blocks, message,
            *landing, *landing,
            pltpu.SemaphoreType.DMA((3,)), pltpu.SemaphoreType.DMA((3,)),
            pltpu.SemaphoreType.DMA((MSGS,)), pltpu.SemaphoreType.DMA((MSGS,)),
            pltpu.SemaphoreType.DMA((4, 8)), pltpu.SemaphoreType.DMA((4, 8)),
        ],
        compiler_params=pltpu.CompilerParams(
            collective_id=0, has_side_effects=True, vmem_limit_bytes=56 * 1024 * 1024
        ),
    )(tokens, cotangent, expert_ids, gate_values, w_gate, w_up, w_down)


def solution(mesh):
    return jax.shard_map(
        body,
        mesh=mesh,
        in_specs=(
            P("dp", "hst"),
            P("dp", "hst"),
            P("dp", None),
            P("dp", None),
            P("hst", "dp", None),
            P("hst", "dp", None),
            P("hst", "dp", None),
        ),
        out_specs=(
            P("dp", "hst"),
            P("dp", "hst"),
            P("hst", "dp", None),
            P("hst", "dp", None),
            P("hst", "dp", None),
        ),
        check_vma=False,
    )
```

```python
import jax
import jax.numpy as jnp
from jax import lax
from jax.experimental import pallas as pl
from jax.experimental.pallas import tpu as pltpu
from jax.sharding import PartitionSpec as P

F32, BF16 = jnp.float32, jnp.bfloat16
HIGHEST = lax.Precision.HIGHEST
MESH = pl.DeviceIdType.MESH
NX, NZ, HOSTS, CAP, TOK = 4, 8, 8, 4, 16
ROWS = NX * CAP
R = NZ * ROWS
FEAT = 896
QL = 2 * FEAT
D = NX * QL
FF = 152
LA = 768
TILES = FEAT // 128
MSGS = 192
PLACE = {0: 0, 1: 1, 7: 2, 2: 3, 6: 4, 3: 5, 5: 6, 4: 7}
CHUNKS = ((0, 16), (16, 32), (48, 32), (80, 32), (112, 16))


def rows(k):
    return pl.ds(ROWS * PLACE[k % NZ], ROWS)


def iota(shape, dim):
    return lax.broadcasted_iota(jnp.int32, shape, dim)


def mm(a, b, ca, cb, precision=None):
    return lax.dot_general(
        a, b, (((ca,), (cb,)), ((), ())), precision=precision, preferred_element_type=F32
    )


def add(total, part):
    total[...] = (total[...].astype(F32) + part[...].astype(F32)).astype(BF16)


def add2(total, one, two):
    parts = one[...].astype(F32) + two[...].astype(F32)
    total[...] = (total[...].astype(F32) + parts).astype(BF16)


class Links:
    def __init__(self, ssem, rsem):
        self.ssem, self.rsem, self.sent = ssem, rsem, []

    def send(self, src, dst, land, dev):
        i = len(self.sent)
        copy = pltpu.make_async_remote_copy(
            src_ref=src, dst_ref=dst, send_sem=self.ssem.at[i], recv_sem=self.rsem.at[i],
            device_id=dev, device_id_type=MESH,
        )
        copy.start()
        self.sent.append(copy)
        return pltpu.make_async_remote_copy(
            src_ref=land, dst_ref=land, send_sem=self.ssem.at[i], recv_sem=self.rsem.at[i],
            device_id=dev, device_id_type=MESH,
        ).wait_recv


def ring_steps(*gens):
    for g in gens:
        next(g, None)


def gather(G, links, place):
    x, xp, xm, xo, dxp, dxm, dxo, dzp, dzm = place

    def straight(rs, lo, hi):
        lanes = pl.ds(lo, hi - lo)
        mine = G.at[x, rs, lanes]
        waits = [
            links.send(mine, mine, G.at[q, rs, lanes], dev)
            for q, dev in ((xm, dxp), (xp, dxm), (xo, dxo))
        ]
        yield
        for wait in waits:
            wait()

    def along_x(rs, lo, hi):
        mid = (lo + hi) // 2
        a, b = pl.ds(lo, mid - lo), pl.ds(mid, hi - mid)
        full = pl.ds(lo, hi - lo)
        mine = G.at[x, rs, full]
        p = links.send(mine, mine, G.at[xm, rs, full], dxp)
        m = links.send(mine, mine, G.at[xp, rs, full], dxm)
        yield
        p()
        f = links.send(G.at[xm, rs, a], G.at[xm, rs, a], G.at[xo, rs, a], dxp)
        m()
        g = links.send(G.at[xp, rs, b], G.at[xp, rs, b], G.at[xo, rs, b], dxm)
        yield
        f()
        g()

    def along_z(q, lo, hi):
        mid = (lo + hi) // 2
        p = m = None
        for s in range(1, NZ // 2 + 1):
            if s > 1:
                p()
            lu = pl.ds(lo, hi - lo) if s < NZ // 2 else pl.ds(lo, mid - lo)
            ld = pl.ds(lo, hi - lo) if s < NZ // 2 else pl.ds(mid, hi - mid)
            there = G.at[q, rows(-s), lu]
            p = links.send(G.at[q, rows(1 - s), lu], there, there, dzp)
            if s > 1:
                m()
            there = G.at[q, rows(s), ld]
            m = links.send(G.at[q, rows(s - 1), ld], there, there, dzm)
            yield
        p()
        m()

    a1 = straight(rows(0), 0, LA)
    b1 = along_z(x, LA, QL)
    b2 = [along_x(pl.ds(lo, n), LA, QL) for lo, n in CHUNKS[:-1]]
    b2.append(straight(pl.ds(*CHUNKS[-1]), LA, QL))
    a2 = [along_z(pl.ds(2 * i, 2), 0, LA) for i in range(2)]
    ring_steps(a1, b1, b2[0])
    yield
    ring_steps(a1, *a2, b1, b2[1])
    yield
    ring_steps(b2[0], *a2, b1, b2[2])
    yield
    ring_steps(b2[1], *a2, b1, b2[3])
    yield
    ring_steps(b2[2], *a2, b1, b2[4])
    yield
    ring_steps(b2[3], *a2)
    yield
    ring_steps(*b2)


def scatter(O, landing, links, place):
    x, xp, xm, xo, dxp, dxm, dxo, dzp, dzm = place
    za, zb, xa, xb, xb1, xb2 = landing

    def straight(rs, lo, hi, land):
        lanes = pl.ds(lo, hi - lo)
        waits = [
            links.send(O.at[q, rs, lanes], land.at[i], land.at[i], dev)
            for i, (q, dev) in enumerate(((xp, dxp), (xm, dxm), (xo, dxo)))
        ]
        yield
        for wait in waits:
            wait()
        total = O.at[x, rs, lanes]
        parts = [land[i].astype(F32) for i in range(3)]
        total[...] = (total[...].astype(F32) + (parts[0] + parts[1] + parts[2])).astype(BF16)

    def along_x(rs, lo, hi):
        mid = (lo + hi) // 2
        n = mid - lo
        a, b = pl.ds(lo, n), pl.ds(mid, n)
        full = pl.ds(lo, hi - lo)
        ha, hb = xb1.at[0, rs], xb1.at[1, rs]
        wa, wb = xb2.at[0, rs], xb2.at[1, rs]
        p = links.send(O.at[xo, rs, a], ha, ha, dxp)
        m = links.send(O.at[xo, rs, b], hb, hb, dxm)
        yield
        p()
        add(O.at[xp, rs, a], ha)
        p = links.send(O.at[xp, rs, full], wa, wa, dxp)
        m()
        add(O.at[xm, rs, b], hb)
        m = links.send(O.at[xm, rs, full], wb, wb, dxm)
        yield
        p()
        m()
        add2(O.at[x, rs, full], wa, wb)

    def along_z(q, lq, lo, hi, land):
        mid = (lo + hi) // 2
        n = mid - lo
        a, b = pl.ds(lo, n), pl.ds(mid, n)
        full = pl.ds(lo, hi - lo)

        def at(d, s):
            ref = land.at[d, s] if lq is None else land.at[d, s, lq]
            if s:
                return ref
            return ref.at[:, pl.ds(0, n)] if lq is None else ref.at[:, :, pl.ds(0, n)]

        far = NZ // 2
        m = links.send(O.at[q, rows(far), a], at(0, 0), at(0, 0), dzm)
        p = links.send(O.at[q, rows(far), b], at(1, 0), at(1, 0), dzp)
        yield
        for s in range(1, far):
            k = far - s
            m()
            add(O.at[q, rows(-k), a if s == 1 else full], at(0, s - 1))
            m = links.send(O.at[q, rows(-k), full], at(0, s), at(0, s), dzm)
            p()
            add(O.at[q, rows(k), b if s == 1 else full], at(1, s - 1))
            p = links.send(O.at[q, rows(k), full], at(1, s), at(1, s), dzp)
            yield
        m()
        p()
        add2(O.at[q, rows(0), full], at(0, far - 1), at(1, far - 1))

    az = [along_z(pl.ds(2 * i, 2), pl.ds(2 * i, 2), 0, LA, za) for i in range(2)]
    bx = [along_x(pl.ds(lo, n), LA, QL) for lo, n in CHUNKS[:-1]]
    bx.append(straight(pl.ds(*CHUNKS[-1]), LA, QL, xb))
    bz = along_z(x, None, LA, QL, zb)
    ax = straight(rows(0), 0, LA, xa)
    ring_steps(*az, bx[4], bx[3], bx[2])
    yield
    ring_steps(bx[4], bz, *az, bx[3], bx[1])
    yield
    ring_steps(*az, bx[3], bz, bx[2], bx[0])
    yield
    ring_steps(*az, bx[2], bz, bx[1])
    yield
    ring_steps(*az, ax, bx[1], bz, bx[0])
    yield
    ring_steps(bx[0], bz, ax)


def kernel(
    tok_ref, cot_ref, ids_ref, gate_ref, wg_hbm, wu_hbm, wd_hbm,
    mixed_ref, gtok_ref, gg_ref, gu_ref, gd_ref,
    wg, wu, wd, gx, gd, oo, ob, accg, accu, accd, act_s, dg_s, du_s, qt, qw,
    msend, mrecv, rsend, rrecv, *rest,
):
    land_o, land_b = rest[0:6], rest[6:12]
    wsem, ssem, rsem, asend, arecv = rest[12:]
    dp, h = lax.axis_index("dp"), lax.axis_index("hst")
    z, x = dp // NX, dp % NX
    xp, xm, xo = (x + 1) % NX, (x + NX - 1) % NX, (x + 2) % NX
    dev = lambda zz, xx, hh: (zz * NX + xx, hh)
    dxp, dxm = dev(z, xp, h), dev(z, xm, h)
    dxo = dev(z, xo, h)
    dzp, dzm = dev((z + 1) % NZ, x, h), dev((z + NZ - 1) % NZ, x, h)
    place = (x, xp, xm, xo, dxp, dxm, dxo, dzp, dzm)
    hq, hr = h // 2, h % 2
    other = x != hq

    loads = [
        pltpu.make_async_copy(src.at[0], dst, wsem.at[i])
        for i, (src, dst) in enumerate(((wg_hbm, wg), (wu_hbm, wu), (wd_hbm, wd)))
    ]
    for load in loads:
        load.start()

    barrier = pltpu.get_barrier_semaphore()

    def greet(device):
        pl.semaphore_signal(barrier, inc=1, device_id=device, device_id_type=MESH)

    turn = (hq - x + NX) % NX
    greet(dzp)
    greet(dzm)
    for k in range(1, HOSTS):
        greet(dev(z, hq, (h + k) % HOSTS))
    for i in range(1, NX):
        for r in range(2):
            greet(dev(z, (hq + i) % NX, 2 * x + r))

    @pl.when(other)
    def _():
        greet(dev(z, hq, h))

        @pl.when(hq != xp)
        def _():
            greet(dxp)

        @pl.when(hq != xm)
        def _():
            greet(dxm)

        @pl.when(hq != xo)
        def _():
            greet(dxo)

    eye = iota((TOK, TOK), 0) == iota((TOK, TOK), 1)

    def column(ref, k):
        return jnp.sum(jnp.where(eye, ref[k : k + 1, :], 0), axis=1, keepdims=True)

    id0, id1 = column(ids_ref, 0), column(ids_ref, 1)
    gate0, gate1 = column(gate_ref, 0), column(gate_ref, 1)
    lane = iota((TOK, HOSTS * CAP), 1)
    expert, slot = lane // CAP, (lane % CAP).astype(F32)
    hit0 = (id0 == expert).astype(F32)
    hit1 = (id1 == expert).astype(F32)
    below = (iota((TOK, TOK), 0) > iota((TOK, TOK), 1)).astype(BF16)
    before = mm(below, (hit0 + hit1).astype(BF16), 1, 0)
    hit0 = jnp.where(before == slot, hit0, 0.0)
    hit1 = jnp.where(before + (id0 == expert).astype(F32) == slot, hit1, 0.0)
    wide = (HOSTS * CAP, HOSTS * 32)
    spread = (
        (iota(wide, 0) // CAP == iota(wide, 1) // 32)
        & (iota(wide, 0) % CAP == iota(wide, 1) % CAP)
    ).astype(F32)
    sel = mm(hit0 + hit1, spread, 1, 0, HIGHEST)
    wei = mm(hit0 * gate0 + hit1 * gate1, spread, 1, 0, HIGHEST)
    big = (8 * TOK, HOSTS * 32)
    tile = iota(big, 0) // TOK
    same = (tile == (iota(big, 1) // CAP) % 8) & (tile < TILES)
    qt[...] = jnp.where(same, jnp.concatenate([sel] * 8, axis=0), 0.0)
    qw[...] = jnp.where(same, jnp.concatenate([wei] * 8, axis=0), 0.0)

    def stacked(ref):
        parts = [ref[:, 128 * j : 128 * j + 128] for j in range(TILES)]
        return jnp.concatenate(parts + [jnp.zeros((TOK, 128), ref.dtype)], axis=0)

    xm_rows = mm(qt[...].astype(BF16), stacked(tok_ref), 0, 0).astype(BF16)
    msend[0] = xm_rows.reshape(HOSTS, 32, 128)
    dm_rows = mm(qw[...], stacked(cot_ref).astype(F32), 0, 0, HIGHEST).astype(BF16)
    msend[1] = dm_rows.reshape(HOSTS, 32, 128)

    sq = (128, 128)
    bi, mi = iota(sq, 0), iota(sq, 1)

    def matches(blk, msg):
        return (
            (blk // 16 == (msg // 4) % 8)
            & ((blk // 4) % 4 == msg // 32)
            & (blk % 4 == msg % 4)
        ).astype(F32).astype(BF16)

    into_block, into_msg = matches(bi, mi), matches(mi, bi)

    pl.semaphore_wait(barrier, 18 - 3 * ((NX - turn) // NX))

    def exchange_out(which):
        copies = []
        for k in range(HOSTS):
            e = (h + k) % HOSTS
            copy = pltpu.make_async_remote_copy(
                src_ref=msend.at[which, e], dst_ref=mrecv.at[which, hr, x],
                send_sem=asend.at[which, k], recv_sem=arecv.at[which, hr * NX + x],
                device_id=dev(z, hq, e), device_id_type=MESH,
            )
            if k:
                copy.start()
            else:
                pl.when(other)(copy.start)
            copies.append(copy)

        @pl.when(jnp.logical_not(other))
        def _():
            mrecv[which, hr, x] = msend[which, h]

        return copies

    def exchange_in(which, block):
        for i in range(NX):
            for r in range(2):
                xi = (x + i) % NX
                land = mrecv.at[which, r, xi]
                copy = pltpu.make_async_remote_copy(
                    src_ref=land, dst_ref=land,
                    send_sem=asend.at[which, 0], recv_sem=arecv.at[which, r * NX + xi],
                    device_id=dev(z, xi, 2 * x + r), device_id_type=MESH,
                )
                if i:
                    copy.wait_recv()
                else:
                    pl.when(2 * x + r != h)(copy.wait_recv)
        for r in range(2):
            got = mm(into_block, mrecv[which, r].reshape(128, 128), 1, 0).astype(BF16)
            for j in range(TILES):
                lo = r * FEAT + 128 * j
                block[x, 0:ROWS, lo : lo + 128] = got[16 * j : 16 * j + 16]

    def return_out(which, block):
        copies = []
        for r in range(2):
            parts = [
                block[x, 0:ROWS, r * FEAT + 128 * j : r * FEAT + 128 * j + 128]
                for j in range(TILES)
            ]
            parts.append(jnp.zeros((ROWS, 128), BF16))
            got = mm(into_msg, jnp.concatenate(parts, axis=0), 1, 0).astype(BF16)
            rsend[which, r] = got.reshape(NX, 32, 128)
        for i in range(NX):
            for r in range(2):
                xi = (x + i) % NX
                copy = pltpu.make_async_remote_copy(
                    src_ref=rsend.at[which, r, xi], dst_ref=rrecv.at[which, h],
                    send_sem=asend.at[2 + which, 2 * i + r], recv_sem=arecv.at[2 + which, h],
                    device_id=dev(z, xi, 2 * x + r), device_id_type=MESH,
                )
                if i:
                    copy.start()
                else:
                    pl.when(2 * x + r != h)(copy.start)
                copies.append(copy)

        @pl.when(jnp.logical_not(other))
        def _():
            rrecv[which, h] = rsend[which, hr, x]

        return copies

    def return_in(which, table, out):
        for k in range(HOSTS):
            e = (h + k) % HOSTS
            land = rrecv.at[which, e]
            copy = pltpu.make_async_remote_copy(
                src_ref=land, dst_ref=land,
                send_sem=asend.at[2 + which, 0], recv_sem=arecv.at[2 + which, e],
                device_id=dev(z, hq, e), device_id_type=MESH,
            )
            if k:
                copy.wait_recv()
            else:
                pl.when(other)(copy.wait_recv)
        got = rrecv[which].reshape(HOSTS * 32, 128).astype(F32)
        res = mm(table[...], got, 1, 0, HIGHEST).astype(BF16)
        for j in range(TILES):
            out[:, 128 * j : 128 * j + 128] = res[16 * j : 16 * j + 16]

    links = Links(ssem, rsem)
    quarter = lambda q: slice(q * QL, (q + 1) * QL)

    def gate_task(q):
        g = mm(gx[q], wg[:, quarter(q)], 1, 1)
        u = mm(gx[q], wu[:, quarter(q)], 1, 1)
        accg[...] = g if q == 0 else accg[...] + g
        accu[...] = u if q == 0 else accu[...] + u

    def act_task():
        g = accg[...]
        act_s[...] = (g * jax.nn.sigmoid(g) * accu[...]).astype(BF16)

    def out_task(q):
        oo[q] = mm(act_s[...], wd[:, quarter(q)], 1, 0).astype(BF16)

    def da_task(q):
        a = mm(gd[q], wd[:, quarter(q)], 1, 1)
        accd[...] = a if q == 0 else accd[...] + a

    def hidden_task():
        g, u, a = accg[...], accu[...], accd[...]
        s = jax.nn.sigmoid(g)
        dg_s[...] = (a * u * s * (1.0 + g * (1.0 - s))).astype(BF16)
        du_s[...] = (a * g * s).astype(BF16)

    def back_task(q):
        part = mm(dg_s[...], wg[:, quarter(q)], 1, 0) + mm(du_s[...], wu[:, quarter(q)], 1, 0)
        ob[q] = part.astype(BF16)

    def grad_task(i, q):
        left, right, out = ((dg_s, gx, gg_ref), (du_s, gx, gu_ref), (act_s, gd, gd_ref))[i]
        out[0, :, quarter(q)] = mm(left[...], right[q], 0, 0).astype(BF16)

    def task(f, *args):
        return lambda: f(*args)

    quarters = range(NX)
    pending = exchange_out(0) + exchange_out(1)
    exchange_in(0, gx)
    run_x = gather(gx, links, place)
    next(run_x)
    exchange_in(1, gd)
    run_d = gather(gd, links, place)
    next(run_d)
    for load in loads:
        load.wait()
    for _ in range(5):
        ring_steps(run_x, run_d)
    ring_steps(run_x)
    for q in quarters:
        gate_task(q)
    ring_steps(run_d)
    act_task()
    for q in quarters:
        out_task(q)
    run_o = scatter(oo, land_o, links, place)
    next(run_o)
    for q in quarters:
        da_task(q)
    hidden_task()
    for q in quarters:
        back_task(q)
    run_b = scatter(ob, land_b, links, place)
    next(run_b)
    tasks = [task(grad_task, i, q) for i in range(3) for q in quarters]
    for _ in range(4):
        ring_steps(run_o, run_b)
        for t in tasks[:3]:
            t()
        tasks = tasks[3:]
    ring_steps(run_o)
    pending += return_out(0, oo)
    ring_steps(run_b)
    pending += return_out(1, ob)
    return_in(0, qw, mixed_ref)
    return_in(1, qt, gtok_ref)

    for copy in links.sent:
        copy.wait_send()
    for n, copy in enumerate(pending):
        first = n < 2 * HOSTS
        if first and n % HOSTS == 0:
            pl.when(other)(copy.wait_send)
        elif not first and n % HOSTS < 2:
            pl.when(2 * x + n % HOSTS != h)(copy.wait_send)
        else:
            copy.wait_send()


def write_out(*refs):
    parts, outs, sem = refs[:5], refs[5:10], refs[10]
    copies = [pltpu.make_async_copy(parts[i], outs[i], sem.at[i]) for i in range(5)]
    for copy in copies:
        copy.start()
    for copy in copies:
        copy.wait()


def body(tokens, cotangent, expert_ids, gate_values, w_gate, w_up, w_down):
    vmem, hbm = pl.BlockSpec(memory_space=pltpu.VMEM), pl.BlockSpec(memory_space=pl.ANY)
    shapes = [(TOK, FEAT)] * 2 + [(1, FF, D)] * 3
    landing = [
        pltpu.VMEM((2, 4, NX, ROWS, LA), BF16),
        pltpu.VMEM((2, 4, ROWS, QL - LA), BF16),
        pltpu.VMEM((3, ROWS, LA), BF16),
        pltpu.VMEM((3, ROWS, QL - LA), BF16),
        pltpu.VMEM((2, R, (QL - LA) // 2), BF16),
        pltpu.VMEM((2, R, QL - LA), BF16),
    ]
    weight, table = pltpu.VMEM((FF, D), BF16), pltpu.VMEM((NX, R, QL), BF16)
    acc, hid = pltpu.VMEM((R, FF), F32), pltpu.VMEM((R, FF), BF16)
    message = pltpu.VMEM((2, HOSTS, 32, 128), BF16)
    blocks = pltpu.VMEM((2, 2, NX, 32, 128), BF16)
    parts = pl.pallas_call(
        kernel,
        out_shape=[pltpu.VMEM(shape, BF16) for shape in shapes],
        in_specs=[vmem] * 4 + [hbm] * 3,
        out_specs=[vmem] * 5,
        scratch_shapes=[
            weight, weight, weight, table, table, table, table, acc, acc, acc, hid, hid, hid,
            pltpu.VMEM((8 * TOK, HOSTS * 32), F32), pltpu.VMEM((8 * TOK, HOSTS * 32), F32),
            message, blocks, blocks, message,
            *landing, *landing,
            pltpu.SemaphoreType.DMA((3,)),
            pltpu.SemaphoreType.DMA((MSGS,)), pltpu.SemaphoreType.DMA((MSGS,)),
            pltpu.SemaphoreType.DMA((4, 8)), pltpu.SemaphoreType.DMA((4, 8)),
        ],
        compiler_params=pltpu.CompilerParams(
            collective_id=0, has_side_effects=True, vmem_limit_bytes=52 * 1024 * 1024
        ),
    )(tokens, cotangent, expert_ids.T, gate_values.T, w_gate, w_up, w_down)
    return pl.pallas_call(
        write_out,
        out_shape=[jax.ShapeDtypeStruct(shape, BF16) for shape in shapes],
        in_specs=[vmem] * 5,
        out_specs=[hbm] * 5,
        scratch_shapes=[pltpu.SemaphoreType.DMA((5,))],
        compiler_params=pltpu.CompilerParams(vmem_limit_bytes=1024 * 1024),
    )(*[pltpu.with_memory_space_constraint(part, pltpu.VMEM) for part in parts])


def solution(mesh):
    return jax.shard_map(
        body,
        mesh=mesh,
        in_specs=(
            P("dp", "hst"),
            P("dp", "hst"),
            P("dp", None),
            P("dp", None),
            P("hst", "dp", None),
            P("hst", "dp", None),
            P("hst", "dp", None),
        ),
        out_specs=(
            P("dp", "hst"),
            P("dp", "hst"),
            P("hst", "dp", None),
            P("hst", "dp", None),
            P("hst", "dp", None),
        ),
        check_vma=False,
    )
```

```python
import jax
import jax.numpy as jnp
from jax import lax
from jax.experimental import pallas as pl
from jax.experimental.pallas import tpu as pltpu
from jax.sharding import PartitionSpec as P

F32, BF16 = jnp.float32, jnp.bfloat16
HIGHEST = lax.Precision.HIGHEST
MESH = pl.DeviceIdType.MESH
NX, NZ, HOSTS, CAP, TOK = 4, 8, 8, 4, 16
ROWS = NX * CAP
R = NZ * ROWS
FEAT = 896
QL = 2 * FEAT
D = NX * QL
FF = 152
LA = 768
TILES = FEAT // 128
MSGS = 54
PLACE = {0: 0, 1: 1, 7: 2, 2: 3, 6: 4, 3: 5, 5: 6, 4: 7}
CHUNKS = ((0, 16), (16, 32), (48, 32), (80, 32), (112, 16))


def rows(k):
    return pl.ds(ROWS * PLACE[k % NZ], ROWS)


def iota(shape, dim):
    return lax.broadcasted_iota(jnp.int32, shape, dim)


def mm(a, b, ca, cb, precision=None):
    return lax.dot_general(
        a, b, (((ca,), (cb,)), ((), ())), precision=precision, preferred_element_type=F32
    )


def add(total, part):
    total[...] = (total[...].astype(F32) + part[...].astype(F32)).astype(BF16)


def add2(total, one, two):
    parts = one[...].astype(F32) + two[...].astype(F32)
    total[...] = (total[...].astype(F32) + parts).astype(BF16)


class Links:
    def __init__(self, ssem, rsem, first):
        self.ssem, self.rsem, self.next = ssem, rsem, first

    def copy(self, src, dst, dev, i, group):
        return pltpu.make_async_remote_copy(
            src_ref=src, dst_ref=dst, send_sem=self.ssem.at[group], recv_sem=self.rsem.at[i],
            device_id=dev, device_id_type=MESH,
        )

    def send(self, src, dst, land, dev, group):
        i = self.next
        self.next += 1
        self.copy(src, dst, dev, i, group).start()
        return self.copy(land, land, dev, i, group).wait_recv

    def wait_sent(self, table, dev):
        for group, ref in ((0, table.at[0, pl.ds(0, 112)]), (1, table.at[pl.ds(0, 3)])):
            self.copy(ref, ref, dev, 0, group).wait_send()


def ring_steps(*gens):
    for g in gens:
        next(g, None)


def gather(G, links, place):
    x, xp, xm, xo, dxp, dxm, dxo, dzp, dzm = place

    def straight(rs, lo, hi):
        lanes = pl.ds(lo, hi - lo)
        mine = G.at[x, rs, lanes]
        waits = [
            links.send(mine, mine, G.at[q, rs, lanes], dev, 1)
            for q, dev in ((xm, dxp), (xp, dxm), (xo, dxo))
        ]
        yield
        for wait in waits:
            wait()

    def along_x(rs, lo, hi):
        mid = (lo + hi) // 2
        a, b = pl.ds(lo, mid - lo), pl.ds(mid, hi - mid)
        full = pl.ds(lo, hi - lo)
        mine = G.at[x, rs, full]
        p = links.send(mine, mine, G.at[xm, rs, full], dxp, 1)
        m = links.send(mine, mine, G.at[xp, rs, full], dxm, 1)
        yield
        p()
        f = links.send(G.at[xm, rs, a], G.at[xm, rs, a], G.at[xo, rs, a], dxp, 1)
        m()
        g = links.send(G.at[xp, rs, b], G.at[xp, rs, b], G.at[xo, rs, b], dxm, 1)
        yield
        f()
        g()

    def along_z(q, lo, hi, group):
        mid = (lo + hi) // 2
        p = m = None
        for s in range(1, NZ // 2 + 1):
            if s > 1:
                p()
            lu = pl.ds(lo, hi - lo) if s < NZ // 2 else pl.ds(lo, mid - lo)
            ld = pl.ds(lo, hi - lo) if s < NZ // 2 else pl.ds(mid, hi - mid)
            there = G.at[q, rows(-s), lu]
            p = links.send(G.at[q, rows(1 - s), lu], there, there, dzp, group)
            if s > 1:
                m()
            there = G.at[q, rows(s), ld]
            m = links.send(G.at[q, rows(s - 1), ld], there, there, dzm, group)
            yield
        p()
        m()

    own = along_z(x, 0, QL, 0)
    a1 = straight(rows(0), 0, LA)
    b2 = [along_x(pl.ds(lo, n), LA, QL) for lo, n in CHUNKS[:-1]]
    b2.append(straight(pl.ds(*CHUNKS[-1]), LA, QL))
    a2 = [along_z(q, 0, LA, 1) for q in (xp, xm, xo)]
    ring_steps(own, a1, b2[0])
    yield
    ring_steps(a1, *a2, own, b2[1], b2[0])
    yield
    ring_steps(own, b2[2], b2[1], *a2)
    yield
    ring_steps(own, b2[3], b2[2], *a2, b2[0])
    yield
    ring_steps(own, b2[4], b2[3], *a2, b2[1])
    yield
    ring_steps(*a2, *b2)


def scatter(O, landing, links, place):
    x, xp, xm, xo, dxp, dxm, dxo, dzp, dzm = place
    za, zb, xa, xb, xb1, xb2 = landing

    def straight(rs, lo, hi, land):
        lanes = pl.ds(lo, hi - lo)
        waits = [
            links.send(O.at[q, rs, lanes], land.at[i], land.at[i], dev, 0)
            for i, (q, dev) in enumerate(((xp, dxp), (xm, dxm), (xo, dxo)))
        ]
        yield
        for wait in waits:
            wait()
        total = O.at[x, rs, lanes]
        parts = [land[i].astype(F32) for i in range(3)]
        total[...] = (total[...].astype(F32) + (parts[0] + parts[1] + parts[2])).astype(BF16)

    def along_x(rs, lo, hi):
        mid = (lo + hi) // 2
        n = mid - lo
        a, b = pl.ds(lo, n), pl.ds(mid, n)
        full = pl.ds(lo, hi - lo)
        ha, hb = xb1.at[0, rs], xb1.at[1, rs]
        wa, wb = xb2.at[0, rs], xb2.at[1, rs]
        p = links.send(O.at[xo, rs, a], ha, ha, dxp, 1)
        m = links.send(O.at[xo, rs, b], hb, hb, dxm, 1)
        yield
        p()
        add(O.at[xp, rs, a], ha)
        p = links.send(O.at[xp, rs, full], wa, wa, dxp, 1)
        m()
        add(O.at[xm, rs, b], hb)
        m = links.send(O.at[xm, rs, full], wb, wb, dxm, 1)
        yield
        p()
        m()
        add2(O.at[x, rs, full], wa, wb)

    def along_z(q, lq, lo, hi, land, group):
        mid = (lo + hi) // 2
        n = mid - lo
        a, b = pl.ds(lo, n), pl.ds(mid, n)
        full = pl.ds(lo, hi - lo)

        def at(d, s):
            ref = land.at[d, s] if lq is None else land.at[d, s, lq]
            if s:
                return ref
            return ref.at[:, pl.ds(0, n)] if lq is None else ref.at[:, :, pl.ds(0, n)]

        far = NZ // 2
        m = links.send(O.at[q, rows(far), a], at(0, 0), at(0, 0), dzm, group)
        p = links.send(O.at[q, rows(far), b], at(1, 0), at(1, 0), dzp, group)
        yield
        for s in range(1, far):
            k = far - s
            m()
            add(O.at[q, rows(-k), a if s == 1 else full], at(0, s - 1))
            m = links.send(O.at[q, rows(-k), full], at(0, s), at(0, s), dzm, group)
            p()
            add(O.at[q, rows(k), b if s == 1 else full], at(1, s - 1))
            p = links.send(O.at[q, rows(k), full], at(1, s), at(1, s), dzp, group)
            yield
        m()
        p()
        add2(O.at[q, rows(0), full], at(0, far - 1), at(1, far - 1))

    az = [along_z(pl.ds(2 * i, 2), pl.ds(2 * i, 2), 0, LA, za, 1) for i in range(2)]
    bx = [along_x(pl.ds(lo, n), LA, QL) for lo, n in CHUNKS[:-1]]
    bx.append(straight(pl.ds(*CHUNKS[-1]), LA, QL, xb))
    bz = along_z(x, None, LA, QL, zb, 0)
    ax = straight(rows(0), 0, LA, xa)
    ring_steps(*az, bx[4], bx[3], bx[2])
    yield
    ring_steps(bx[4], bz, *az, bx[3], bx[1])
    yield
    ring_steps(*az, bx[3], bz, bx[2], bx[0])
    yield
    ring_steps(*az, bx[2], bz, bx[1])
    yield
    ring_steps(*az, ax, bx[1], bz, bx[0])
    yield
    ring_steps(bx[0], bz, ax)


def kernel(
    tok_hbm, cot_hbm, ids_hbm, gate_hbm, wg_hbm, wu_hbm, wd_hbm,
    mixed_ref, gtok_ref, gg_ref, gu_ref, gd_ref,
    tok_ref, cot_ref, ids_ref, gate_ref, wg, wu, wd, gx, gd, oo, ob, accg, accu, accd, act_s, dg_s, du_s, qt, qw,
    msend, mrecv, rsend, rrecv, *rest,
):
    land_o, land_b = rest[0:6], rest[6:12]
    wsem, ssem, rsem, asend, arecv = rest[12:]
    dp, h = lax.axis_index("dp"), lax.axis_index("hst")
    z, x = dp // NX, dp % NX
    xp, xm, xo = (x + 1) % NX, (x + NX - 1) % NX, (x + 2) % NX
    dev = lambda zz, xx, hh: (zz * NX + xx, hh)
    dxp, dxm = dev(z, xp, h), dev(z, xm, h)
    dxo = dev(z, xo, h)
    dzp, dzm = dev((z + 1) % NZ, x, h), dev((z + NZ - 1) % NZ, x, h)
    hq, hr = h // 2, h % 2
    own = (x - hq + NX) % NX
    turned = [(own + i) % NX for i in (0, 1, NX - 1, 2)]
    place = (*turned, dxp, dxm, dxo, dzp, dzm)
    other = own != hq
    owner = lambda e: dev(z, (hq + e // 2) % NX, e)
    source = lambda xx, r: dev(z, xx, 2 * own + r)

    small = ((ids_hbm, ids_ref), (gate_hbm, gate_ref), (tok_hbm, tok_ref), (cot_hbm, cot_ref))
    large = ((wg_hbm.at[0], wg), (wu_hbm.at[0], wu), (wd_hbm.at[0], wd))
    loads = [
        pltpu.make_async_copy(src, dst, wsem.at[i]) for i, (src, dst) in enumerate(small + large)
    ]
    for load in loads:
        load.start()

    barrier = pltpu.get_barrier_semaphore()

    def greet(device):
        pl.semaphore_signal(barrier, inc=1, device_id=device, device_id_type=MESH)

    turn = (hq - own + NX) % NX
    greet(dzp)
    greet(dzm)
    for k in range(1, HOSTS):
        greet(owner((h + k) % HOSTS))
    for i in range(1, NX):
        for r in range(2):
            greet(source((x + i) % NX, r))

    @pl.when(other)
    def _():
        greet(owner(h))

        @pl.when(turn != 1)
        def _():
            greet(dxp)

        @pl.when(turn != 3)
        def _():
            greet(dxm)

        @pl.when(turn != 2)
        def _():
            greet(dxo)

    for load in loads[:4]:
        load.wait()
    eye = iota((TOK, TOK), 0) == iota((TOK, TOK), 1)

    def column(ref, k):
        return jnp.sum(jnp.where(eye, ref[k : k + 1, :], 0), axis=1, keepdims=True)

    id0, id1 = column(ids_ref, 0), column(ids_ref, 1)
    gate0, gate1 = column(gate_ref, 0), column(gate_ref, 1)
    lane = iota((TOK, HOSTS * CAP), 1)
    expert, slot = lane // CAP, (lane % CAP).astype(F32)
    hit0 = (id0 == expert).astype(F32)
    hit1 = (id1 == expert).astype(F32)
    below = (iota((TOK, TOK), 0) > iota((TOK, TOK), 1)).astype(BF16)
    before = mm(below, (hit0 + hit1).astype(BF16), 1, 0)
    hit0 = jnp.where(before == slot, hit0, 0.0)
    hit1 = jnp.where(before + (id0 == expert).astype(F32) == slot, hit1, 0.0)
    wide = (HOSTS * CAP, HOSTS * 32)
    spread = (
        (iota(wide, 0) // CAP == iota(wide, 1) // 32)
        & (iota(wide, 0) % CAP == iota(wide, 1) % CAP)
    ).astype(F32)
    sel = mm(hit0 + hit1, spread, 1, 0, HIGHEST)
    wei = mm(hit0 * gate0 + hit1 * gate1, spread, 1, 0, HIGHEST)
    big = (8 * TOK, HOSTS * 32)
    tile = iota(big, 0) // TOK
    same = (tile == (iota(big, 1) // CAP) % 8) & (tile < TILES)
    qt[...] = jnp.where(same, jnp.concatenate([sel] * 8, axis=0), 0.0)
    qw[...] = jnp.where(same, jnp.concatenate([wei] * 8, axis=0), 0.0)

    def stacked(ref):
        parts = [ref[:, 128 * j : 128 * j + 128] for j in range(TILES)]
        return jnp.concatenate(parts + [jnp.zeros((TOK, 128), ref.dtype)], axis=0)

    xm_rows = mm(qt[...].astype(BF16), stacked(tok_ref), 0, 0).astype(BF16)
    msend[:, 0:32] = xm_rows.reshape(HOSTS, 32, 128)
    dm_rows = mm(qw[...], stacked(cot_ref).astype(F32), 0, 0, HIGHEST).astype(BF16)
    msend[:, 32:64] = dm_rows.reshape(HOSTS, 32, 128)

    sq = (128, 128)
    bi, mi = iota(sq, 0), iota(sq, 1)

    def matches(blk, msg):
        return (
            (blk // 16 == (msg // 4) % 8)
            & ((blk // 4) % 4 == msg // 32)
            & (blk % 4 == msg % 4)
        ).astype(F32).astype(BF16)

    into_block, into_msg = matches(bi, mi), matches(mi, bi)

    pl.semaphore_wait(barrier, 18 - 3 * ((NX - turn) // NX))

    def exchange_out():
        for k in range(HOSTS):
            e = (h + k) % HOSTS
            copy = pltpu.make_async_remote_copy(
                src_ref=msend.at[e], dst_ref=mrecv.at[hr, x],
                send_sem=asend.at[0, min(k, 1)], recv_sem=arecv.at[0, hr * NX + x],
                device_id=owner(e), device_id_type=MESH,
            )
            if k:
                copy.start()
            else:
                pl.when(other)(copy.start)

        @pl.when(jnp.logical_not(other))
        def _():
            mrecv[hr, x] = msend[h]

    def exchange_in():
        for i in range(NX):
            for r in range(2):
                xi = (x + i) % NX
                land = mrecv.at[r, xi]
                copy = pltpu.make_async_remote_copy(
                    src_ref=land, dst_ref=land,
                    send_sem=asend.at[0, 0], recv_sem=arecv.at[0, r * NX + xi],
                    device_id=source(xi, r), device_id_type=MESH,
                )
                if i:
                    copy.wait_recv()
                else:
                    pl.when(2 * own + r != h)(copy.wait_recv)

    def assemble(which, block):
        for r in range(2):
            got = mrecv[r, :, 32 * which : 32 * which + 32].reshape(128, 128)
            got = mm(into_block, got, 1, 0).astype(BF16)
            for j in range(TILES):
                lo = r * FEAT + 128 * j
                block[own, 0:ROWS, lo : lo + 128] = got[16 * j : 16 * j + 16]

    def return_out(which, block):
        for r in range(2):
            parts = [
                block[own, 0:ROWS, r * FEAT + 128 * j : r * FEAT + 128 * j + 128]
                for j in range(TILES)
            ]
            parts.append(jnp.zeros((ROWS, 128), BF16))
            got = mm(into_msg, jnp.concatenate(parts, axis=0), 1, 0).astype(BF16)
            rsend[which, r] = got.reshape(NX, 32, 128)
        for i in range(NX):
            for r in range(2):
                xi = (x + i) % NX
                copy = pltpu.make_async_remote_copy(
                    src_ref=rsend.at[which, r, xi], dst_ref=rrecv.at[which, h],
                    send_sem=asend.at[1 + which, 2 if i else r], recv_sem=arecv.at[1 + which, h],
                    device_id=source(xi, r), device_id_type=MESH,
                )
                if i:
                    copy.start()
                else:
                    pl.when(2 * own + r != h)(copy.start)

        @pl.when(jnp.logical_not(other))
        def _():
            rrecv[which, h] = rsend[which, hr, x]

    def return_in(which, table, out):
        for k in range(HOSTS):
            e = (h + k) % HOSTS
            land = rrecv.at[which, e]
            copy = pltpu.make_async_remote_copy(
                src_ref=land, dst_ref=land,
                send_sem=asend.at[1 + which, 0], recv_sem=arecv.at[1 + which, e],
                device_id=owner(e), device_id_type=MESH,
            )
            if k:
                copy.wait_recv()
            else:
                pl.when(other)(copy.wait_recv)
        got = rrecv[which].reshape(HOSTS * 32, 128).astype(F32)
        res = mm(table[...], got, 1, 0, HIGHEST).astype(BF16)
        for j in range(TILES):
            out[:, 128 * j : 128 * j + 128] = res[16 * j : 16 * j + 16]

    links = [Links(ssem.at[i], rsem, MSGS * (i % 2)) for i in range(4)]
    quarter = lambda q: slice(q * QL, (q + 1) * QL)

    def gate_task(q):
        g = mm(gx[q], wg[:, quarter(q)], 1, 1)
        u = mm(gx[q], wu[:, quarter(q)], 1, 1)
        accg[...] = g if q == 0 else accg[...] + g
        accu[...] = u if q == 0 else accu[...] + u

    def act_task():
        g = accg[...]
        act_s[...] = (g * jax.nn.sigmoid(g) * accu[...]).astype(BF16)

    def out_task(q):
        oo[q] = mm(act_s[...], wd[:, quarter(q)], 1, 0).astype(BF16)

    def da_task(q):
        a = mm(gd[q], wd[:, quarter(q)], 1, 1)
        accd[...] = a if q == 0 else accd[...] + a

    def hidden_task():
        g, u, a = accg[...], accu[...], accd[...]
        s = jax.nn.sigmoid(g)
        dg_s[...] = (a * u * s * (1.0 + g * (1.0 - s))).astype(BF16)
        du_s[...] = (a * g * s).astype(BF16)

    def back_task(q):
        part = mm(dg_s[...], wg[:, quarter(q)], 1, 0) + mm(du_s[...], wu[:, quarter(q)], 1, 0)
        ob[q] = part.astype(BF16)

    def grad_task(i, q):
        left, right, out = ((dg_s, gx, gg_ref), (du_s, gx, gu_ref), (act_s, gd, gd_ref))[i]
        out[0, :, quarter(q)] = mm(left[...], right[q], 0, 0).astype(BF16)

    def task(f, *args):
        return lambda: f(*args)

    quarters = range(NX)
    exchange_out()
    exchange_in()
    assemble(0, gx)
    run_x = gather(gx, links[0], place)
    next(run_x)
    assemble(1, gd)
    run_d = gather(gd, links[1], place)
    next(run_d)
    for load in loads[4:]:
        load.wait()
    for _ in range(4):
        ring_steps(run_x, run_d)
    ring_steps(run_x)
    for q in quarters:
        gate_task(q)
    act_task()
    for q in quarters:
        out_task(q)
    run_o = scatter(oo, land_o, links[3], place)
    next(run_o)
    ring_steps(run_d)
    for q in quarters:
        da_task(q)
    hidden_task()
    for q in quarters:
        back_task(q)
    run_b = scatter(ob, land_b, links[2], place)
    next(run_b)
    tasks = [task(grad_task, i, q) for i in range(3) for q in quarters]
    for _ in range(4):
        ring_steps(run_o, run_b)
        for t in tasks[:3]:
            t()
        tasks = tasks[3:]
    ring_steps(run_o)
    return_out(0, oo)
    ring_steps(run_b)
    return_out(1, ob)
    return_in(0, qw, mixed_ref)
    return_in(1, qt, gtok_ref)

    for i, table in enumerate((gx, gd, ob, oo)):
        links[i].wait_sent(table, dzp)

    def wait_sent(ref, sem):
        pltpu.make_async_remote_copy(
            src_ref=ref, dst_ref=ref, send_sem=sem, recv_sem=arecv.at[0, 0],
            device_id=dzp, device_id_type=MESH,
        ).wait_send()

    wait_sent(msend.at[pl.ds(1, HOSTS - 1)], asend.at[0, 1])

    @pl.when(other)
    def _():
        wait_sent(msend.at[0], asend.at[0, 0])

    for which in range(2):
        wait_sent(rsend.at[which, :, pl.ds(1, NX - 1)], asend.at[1 + which, 2])
        for r in range(2):

            @pl.when(2 * own + r != h)
            def _():
                wait_sent(rsend.at[which, r, 0], asend.at[1 + which, r])


def write_out(*refs):
    parts, outs, sem = refs[:5], refs[5:10], refs[10]
    copies = [pltpu.make_async_copy(parts[i], outs[i], sem.at[i]) for i in range(5)]
    for copy in copies:
        copy.start()
    for copy in copies:
        copy.wait()


def body(tokens, cotangent, expert_ids, gate_values, w_gate, w_up, w_down):
    vmem, hbm = pl.BlockSpec(memory_space=pltpu.VMEM), pl.BlockSpec(memory_space=pl.ANY)
    shapes = [(TOK, FEAT)] * 2 + [(1, FF, D)] * 3
    landing = [
        pltpu.VMEM((2, 4, NX, ROWS, LA), BF16),
        pltpu.VMEM((2, 4, ROWS, QL - LA), BF16),
        pltpu.VMEM((3, ROWS, LA), BF16),
        pltpu.VMEM((3, ROWS, QL - LA), BF16),
        pltpu.VMEM((2, R, (QL - LA) // 2), BF16),
        pltpu.VMEM((2, R, QL - LA), BF16),
    ]
    weight, table = pltpu.VMEM((FF, D), BF16), pltpu.VMEM((NX, R, QL), BF16)
    acc, hid = pltpu.VMEM((R, FF), F32), pltpu.VMEM((R, FF), BF16)
    parts = pl.pallas_call(
        kernel,
        out_shape=[pltpu.VMEM(shape, BF16) for shape in shapes],
        in_specs=[hbm] * 7,
        out_specs=[vmem] * 5,
        scratch_shapes=[
            pltpu.VMEM((TOK, FEAT), BF16), pltpu.VMEM((TOK, FEAT), BF16),
            pltpu.VMEM((2, TOK), jnp.int32), pltpu.VMEM((2, TOK), F32),
            weight, weight, weight, table, table, table, table, acc, acc, acc, hid, hid, hid,
            pltpu.VMEM((8 * TOK, HOSTS * 32), F32), pltpu.VMEM((8 * TOK, HOSTS * 32), F32),
            pltpu.VMEM((HOSTS, 64, 128), BF16), pltpu.VMEM((2, NX, 64, 128), BF16),
            pltpu.VMEM((2, 2, NX, 32, 128), BF16), pltpu.VMEM((2, HOSTS, 32, 128), BF16),
            *landing, *landing,
            pltpu.SemaphoreType.DMA((7,)),
            pltpu.SemaphoreType.DMA((4, 2)), pltpu.SemaphoreType.DMA((2 * MSGS,)),
            pltpu.SemaphoreType.DMA((3, 3)), pltpu.SemaphoreType.DMA((3, 8)),
        ],
        compiler_params=pltpu.CompilerParams(
            collective_id=0, has_side_effects=True, vmem_limit_bytes=52 * 1024 * 1024
        ),
    )(tokens, cotangent, expert_ids.T, gate_values.T, w_gate, w_up, w_down)
    return pl.pallas_call(
        write_out,
        out_shape=[jax.ShapeDtypeStruct(shape, BF16) for shape in shapes],
        in_specs=[vmem] * 5,
        out_specs=[hbm] * 5,
        scratch_shapes=[pltpu.SemaphoreType.DMA((5,))],
        compiler_params=pltpu.CompilerParams(vmem_limit_bytes=1024 * 1024),
    )(*[pltpu.with_memory_space_constraint(part, pltpu.VMEM) for part in parts])


def solution(mesh):
    return jax.shard_map(
        body,
        mesh=mesh,
        in_specs=(
            P("dp", "hst"),
            P("dp", "hst"),
            P("dp", None),
            P("dp", None),
            P("hst", "dp", None),
            P("hst", "dp", None),
            P("hst", "dp", None),
        ),
        out_specs=(
            P("dp", "hst"),
            P("dp", "hst"),
            P("hst", "dp", None),
            P("hst", "dp", None),
            P("hst", "dp", None),
        ),
        check_vma=False,
    )
```

```python
import jax
import jax.numpy as jnp
from jax import lax
from jax.experimental import pallas as pl
from jax.experimental.pallas import tpu as pltpu
from jax.sharding import PartitionSpec as P

F32, BF16 = jnp.float32, jnp.bfloat16
HIGHEST = lax.Precision.HIGHEST
MESH = pl.DeviceIdType.MESH
NX, NZ, HOSTS, CAP, TOK = 4, 8, 8, 4, 16
ROWS = NX * CAP
R = NZ * ROWS
FEAT = 896
QL = 2 * FEAT
D = NX * QL
FF = 152
LA = 768
TILES = FEAT // 128
MSGS = 54
PLACE = {0: 0, 1: 1, 7: 2, 2: 3, 6: 4, 3: 5, 5: 6, 4: 7}
CHUNKS = ((0, 16), (16, 32), (48, 32), (80, 32), (112, 16))


def rows(k):
    return pl.ds(ROWS * PLACE[k % NZ], ROWS)


def iota(shape, dim):
    return lax.broadcasted_iota(jnp.int32, shape, dim)


def mm(a, b, ca, cb, precision=None):
    return lax.dot_general(
        a, b, (((ca,), (cb,)), ((), ())), precision=precision, preferred_element_type=F32
    )


def add(total, part):
    total[...] = (total[...].astype(F32) + part[...].astype(F32)).astype(BF16)


def add2(total, one, two):
    parts = one[...].astype(F32) + two[...].astype(F32)
    total[...] = (total[...].astype(F32) + parts).astype(BF16)


class Links:
    def __init__(self, ssem, rsem, first):
        self.ssem, self.rsem, self.next = ssem, rsem, first

    def copy(self, src, dst, dev, i, group):
        return pltpu.make_async_remote_copy(
            src_ref=src, dst_ref=dst, send_sem=self.ssem.at[group], recv_sem=self.rsem.at[i],
            device_id=dev, device_id_type=MESH,
        )

    def send(self, src, dst, land, dev, group):
        i = self.next
        self.next += 1
        self.copy(src, dst, dev, i, group).start()
        return self.copy(land, land, dev, i, group).wait_recv

    def wait_sent(self, table, dev):
        for group, ref in ((0, table.at[0, pl.ds(0, 112)]), (1, table.at[pl.ds(0, 3)])):
            self.copy(ref, ref, dev, 0, group).wait_send()


def ring_steps(*gens):
    for g in gens:
        next(g, None)


def gather(G, links, place):
    x, xp, xm, xo, dxp, dxm, dxo, dzp, dzm = place

    def straight(rs, lo, hi):
        lanes = pl.ds(lo, hi - lo)
        mine = G.at[x, rs, lanes]
        waits = [
            links.send(mine, mine, G.at[q, rs, lanes], dev, 1)
            for q, dev in ((xo, dxo), (xm, dxp), (xp, dxm))
        ]
        yield
        for wait in waits:
            wait()

    def along_x(rs, lo, hi):
        mid = (lo + hi) // 2
        a, b = pl.ds(lo, mid - lo), pl.ds(mid, hi - mid)
        full = pl.ds(lo, hi - lo)
        mine = G.at[x, rs, full]
        p = links.send(mine, mine, G.at[xm, rs, full], dxp, 1)
        m = links.send(mine, mine, G.at[xp, rs, full], dxm, 1)
        yield
        p()
        f = links.send(G.at[xm, rs, a], G.at[xm, rs, a], G.at[xo, rs, a], dxp, 1)
        m()
        g = links.send(G.at[xp, rs, b], G.at[xp, rs, b], G.at[xo, rs, b], dxm, 1)
        yield
        f()
        g()

    def along_z(q, lo, hi, group):
        mid = (lo + hi) // 2
        p = m = None
        for s in range(1, NZ // 2 + 1):
            if s > 1:
                p()
            lu = pl.ds(lo, hi - lo) if s < NZ // 2 else pl.ds(lo, mid - lo)
            ld = pl.ds(lo, hi - lo) if s < NZ // 2 else pl.ds(mid, hi - mid)
            there = G.at[q, rows(-s), lu]
            p = links.send(G.at[q, rows(1 - s), lu], there, there, dzp, group)
            if s > 1:
                m()
            there = G.at[q, rows(s), ld]
            m = links.send(G.at[q, rows(s - 1), ld], there, there, dzm, group)
            yield
        p()
        m()

    own = along_z(x, 0, QL, 0)
    a1 = straight(rows(0), 0, LA)
    b2 = [along_x(pl.ds(lo, n), LA, QL) for lo, n in CHUNKS[:-1]]
    b2.append(straight(pl.ds(*CHUNKS[-1]), LA, QL))
    a2 = [along_z(q, 0, LA, 1) for q in (xp, xm, xo)]
    ring_steps(own, a1, b2[0])
    yield
    ring_steps(a1, *a2, own, b2[1], b2[0])
    yield
    ring_steps(own, b2[2], b2[1], *a2)
    yield
    ring_steps(own, b2[3], b2[2], *a2, b2[0])
    yield
    ring_steps(own, b2[4], b2[3], *a2, b2[1])
    yield
    ring_steps(*a2, *b2)


def scatter(O, landing, links, place):
    x, xp, xm, xo, dxp, dxm, dxo, dzp, dzm = place
    za, zb, xa, xb, xb1, xb2 = landing

    def straight(rs, lo, hi, land):
        lanes = pl.ds(lo, hi - lo)
        waits = [
            links.send(O.at[q, rs, lanes], land.at[i], land.at[i], dev, 0)
            for i, (q, dev) in enumerate(((xo, dxo), (xp, dxp), (xm, dxm)))
        ]
        yield
        for wait in waits:
            wait()
        total = O.at[x, rs, lanes]
        parts = [land[i].astype(F32) for i in range(3)]
        total[...] = (total[...].astype(F32) + (parts[0] + parts[1] + parts[2])).astype(BF16)

    def along_x(rs, lo, hi):
        mid = (lo + hi) // 2
        n = mid - lo
        a, b = pl.ds(lo, n), pl.ds(mid, n)
        full = pl.ds(lo, hi - lo)
        ha, hb = xb1.at[0, rs], xb1.at[1, rs]
        wa, wb = xb2.at[0, rs], xb2.at[1, rs]
        p = links.send(O.at[xo, rs, a], ha, ha, dxp, 1)
        m = links.send(O.at[xo, rs, b], hb, hb, dxm, 1)
        yield
        p()
        add(O.at[xp, rs, a], ha)
        p = links.send(O.at[xp, rs, full], wa, wa, dxp, 1)
        m()
        add(O.at[xm, rs, b], hb)
        m = links.send(O.at[xm, rs, full], wb, wb, dxm, 1)
        yield
        p()
        m()
        add2(O.at[x, rs, full], wa, wb)

    def along_z(q, lq, lo, hi, land, group):
        mid = (lo + hi) // 2
        n = mid - lo
        a, b = pl.ds(lo, n), pl.ds(mid, n)
        full = pl.ds(lo, hi - lo)

        def at(d, s):
            ref = land.at[d, s] if lq is None else land.at[d, s, lq]
            if s:
                return ref
            return ref.at[:, pl.ds(0, n)] if lq is None else ref.at[:, :, pl.ds(0, n)]

        far = NZ // 2
        m = links.send(O.at[q, rows(far), a], at(0, 0), at(0, 0), dzm, group)
        p = links.send(O.at[q, rows(far), b], at(1, 0), at(1, 0), dzp, group)
        yield
        for s in range(1, far):
            k = far - s
            m()
            add(O.at[q, rows(-k), a if s == 1 else full], at(0, s - 1))
            m = links.send(O.at[q, rows(-k), full], at(0, s), at(0, s), dzm, group)
            p()
            add(O.at[q, rows(k), b if s == 1 else full], at(1, s - 1))
            p = links.send(O.at[q, rows(k), full], at(1, s), at(1, s), dzp, group)
            yield
        m()
        p()
        add2(O.at[q, rows(0), full], at(0, far - 1), at(1, far - 1))

    az = [along_z(pl.ds(2 * i, 2), pl.ds(2 * i, 2), 0, LA, za, 1) for i in range(2)]
    bx = [along_x(pl.ds(lo, n), LA, QL) for lo, n in CHUNKS[:-1]]
    bx.append(straight(pl.ds(*CHUNKS[-1]), LA, QL, xb))
    bz = along_z(x, None, LA, QL, zb, 0)
    ax = straight(rows(0), 0, LA, xa)
    ring_steps(*az)
    yield
    ring_steps(bx[4], bx[3])
    yield
    ring_steps(bx[2])
    yield
    ring_steps(*az)
    yield
    ring_steps(bx[4], bz, bx[3])
    yield
    ring_steps(bx[1])
    yield
    ring_steps(*az)
    yield
    ring_steps(bx[3], bz, bx[2])
    yield
    ring_steps(bx[0])
    yield
    ring_steps(*az)
    yield
    ring_steps(bx[2], bz, bx[1])
    yield
    ring_steps(*az, ax)
    yield
    ring_steps(bx[1], bz, bx[0])
    yield
    ring_steps(bx[0], ax, bz)


def kernel(
    tok_hbm, cot_hbm, ids_hbm, gate_hbm, wg_hbm, wu_hbm, wd_hbm,
    mixed_ref, gtok_ref, gg_ref, gu_ref, gd_ref,
    tok_ref, cot_ref, ids_ref, gate_ref, wg, wu, wd, gx, gd, oo, ob, accg, accu, accd, act_s, dg_s, du_s, qt, qw,
    msend, mrecv, rsend, rrecv, *rest,
):
    land_o, land_b = rest[0:6], rest[6:12]
    wsem, ssem, rsem, asend, arecv = rest[12:]
    dp, h = lax.axis_index("dp"), lax.axis_index("hst")
    z, x = dp // NX, dp % NX
    xp, xm, xo = (x + 1) % NX, (x + NX - 1) % NX, (x + 2) % NX
    dev = lambda zz, xx, hh: (zz * NX + xx, hh)
    dxp, dxm = dev(z, xp, h), dev(z, xm, h)
    dxo = dev(z, xo, h)
    dzp, dzm = dev((z + 1) % NZ, x, h), dev((z + NZ - 1) % NZ, x, h)
    hq, hr = h // 2, h % 2
    own = (x - hq + NX) % NX
    turned = [(own + i) % NX for i in (0, 1, NX - 1, 2)]
    place = (*turned, dxp, dxm, dxo, dzp, dzm)
    other = own != hq
    owner = lambda e: dev(z, (hq + e // 2) % NX, e)
    source = lambda xx, r: dev(z, xx, 2 * own + r)

    small = ((ids_hbm, ids_ref), (gate_hbm, gate_ref), (tok_hbm, tok_ref), (cot_hbm, cot_ref))
    large = ((wg_hbm.at[0], wg), (wu_hbm.at[0], wu), (wd_hbm.at[0], wd))
    loads = [
        pltpu.make_async_copy(src, dst, wsem.at[i]) for i, (src, dst) in enumerate(small + large)
    ]
    for load in loads:
        load.start()

    barrier = pltpu.get_barrier_semaphore()

    def greet(device):
        pl.semaphore_signal(barrier, inc=1, device_id=device, device_id_type=MESH)

    turn = (hq - own + NX) % NX
    greet(dzp)
    greet(dzm)
    for k in range(1, HOSTS):
        greet(owner((h + k) % HOSTS))
    for i in range(1, NX):
        for r in range(2):
            greet(source((x + i) % NX, r))

    @pl.when(other)
    def _():
        greet(owner(h))

        @pl.when(turn != 1)
        def _():
            greet(dxp)

        @pl.when(turn != 3)
        def _():
            greet(dxm)

        @pl.when(turn != 2)
        def _():
            greet(dxo)

    for load in loads[:4]:
        load.wait()
    eye = iota((TOK, TOK), 0) == iota((TOK, TOK), 1)

    def column(ref, k):
        return jnp.sum(jnp.where(eye, ref[k : k + 1, :], 0), axis=1, keepdims=True)

    id0, id1 = column(ids_ref, 0), column(ids_ref, 1)
    gate0, gate1 = column(gate_ref, 0), column(gate_ref, 1)
    lane = iota((TOK, HOSTS * CAP), 1)
    expert, slot = lane // CAP, (lane % CAP).astype(F32)
    hit0 = (id0 == expert).astype(F32)
    hit1 = (id1 == expert).astype(F32)
    below = (iota((TOK, TOK), 0) > iota((TOK, TOK), 1)).astype(BF16)
    before = mm(below, (hit0 + hit1).astype(BF16), 1, 0)
    hit0 = jnp.where(before == slot, hit0, 0.0)
    hit1 = jnp.where(before + (id0 == expert).astype(F32) == slot, hit1, 0.0)
    wide = (HOSTS * CAP, HOSTS * 32)
    spread = (
        (iota(wide, 0) // CAP == iota(wide, 1) // 32)
        & (iota(wide, 0) % CAP == iota(wide, 1) % CAP)
    ).astype(F32)
    sel = mm(hit0 + hit1, spread, 1, 0, HIGHEST)
    wei = mm(hit0 * gate0 + hit1 * gate1, spread, 1, 0, HIGHEST)
    big = (8 * TOK, HOSTS * 32)
    tile = iota(big, 0) // TOK
    same = (tile == (iota(big, 1) // CAP) % 8) & (tile < TILES)
    qt[...] = jnp.where(same, jnp.concatenate([sel] * 8, axis=0), 0.0)
    qw[...] = jnp.where(same, jnp.concatenate([wei] * 8, axis=0), 0.0)

    def stacked(ref):
        parts = [ref[:, 128 * j : 128 * j + 128] for j in range(TILES)]
        return jnp.concatenate(parts + [jnp.zeros((TOK, 128), ref.dtype)], axis=0)

    xm_rows = mm(qt[...].astype(BF16), stacked(tok_ref), 0, 0).astype(BF16)
    msend[:, 0:32] = xm_rows.reshape(HOSTS, 32, 128)
    dm_rows = mm(qw[...], stacked(cot_ref).astype(F32), 0, 0, HIGHEST).astype(BF16)
    msend[:, 32:64] = dm_rows.reshape(HOSTS, 32, 128)

    sq = (128, 128)
    bi, mi = iota(sq, 0), iota(sq, 1)

    def matches(blk, msg):
        return (
            (blk // 16 == (msg // 4) % 8)
            & ((blk // 4) % 4 == msg // 32)
            & (blk % 4 == msg % 4)
        ).astype(F32).astype(BF16)

    into_block, into_msg = matches(bi, mi), matches(mi, bi)

    pl.semaphore_wait(barrier, 18 - 3 * ((NX - turn) // NX))

    def exchange_out():
        for k in (4, 3, 5, 2, 6, 1, 7, 0):
            e = (h + k) % HOSTS
            copy = pltpu.make_async_remote_copy(
                src_ref=msend.at[e], dst_ref=mrecv.at[hr, x],
                send_sem=asend.at[0, min(k, 1)], recv_sem=arecv.at[0, hr * NX + x],
                device_id=owner(e), device_id_type=MESH,
            )
            if k:
                copy.start()
            else:
                pl.when(other)(copy.start)

        @pl.when(jnp.logical_not(other))
        def _():
            mrecv[hr, x] = msend[h]

    def exchange_in():
        for i in range(NX):
            for r in range(2):
                xi = (x + i) % NX
                land = mrecv.at[r, xi]
                copy = pltpu.make_async_remote_copy(
                    src_ref=land, dst_ref=land,
                    send_sem=asend.at[0, 0], recv_sem=arecv.at[0, r * NX + xi],
                    device_id=source(xi, r), device_id_type=MESH,
                )
                if i:
                    copy.wait_recv()
                else:
                    pl.when(2 * own + r != h)(copy.wait_recv)

    def assemble(which, block):
        for r in range(2):
            got = mrecv[r, :, 32 * which : 32 * which + 32].reshape(128, 128)
            got = mm(into_block, got, 1, 0).astype(BF16)
            for j in range(TILES):
                lo = r * FEAT + 128 * j
                block[own, 0:ROWS, lo : lo + 128] = got[16 * j : 16 * j + 16]

    def return_out(which, block):
        for r in range(2):
            parts = [
                block[own, 0:ROWS, r * FEAT + 128 * j : r * FEAT + 128 * j + 128]
                for j in range(TILES)
            ]
            parts.append(jnp.zeros((ROWS, 128), BF16))
            got = mm(into_msg, jnp.concatenate(parts, axis=0), 1, 0).astype(BF16)
            rsend[which, r] = got.reshape(NX, 32, 128)
        for i in (2, 1, 3, 0):
            for r in range(2):
                xi = (x + i) % NX
                copy = pltpu.make_async_remote_copy(
                    src_ref=rsend.at[which, r, xi], dst_ref=rrecv.at[which, h],
                    send_sem=asend.at[1 + which, 2 if i else r], recv_sem=arecv.at[1 + which, h],
                    device_id=source(xi, r), device_id_type=MESH,
                )
                if i:
                    copy.start()
                else:
                    pl.when(2 * own + r != h)(copy.start)

        @pl.when(jnp.logical_not(other))
        def _():
            rrecv[which, h] = rsend[which, hr, x]

    def return_in(which, table, out):
        for k in range(HOSTS):
            e = (h + k) % HOSTS
            land = rrecv.at[which, e]
            copy = pltpu.make_async_remote_copy(
                src_ref=land, dst_ref=land,
                send_sem=asend.at[1 + which, 0], recv_sem=arecv.at[1 + which, e],
                device_id=owner(e), device_id_type=MESH,
            )
            if k:
                copy.wait_recv()
            else:
                pl.when(other)(copy.wait_recv)
        got = rrecv[which].reshape(HOSTS * 32, 128)
        if which:
            res = mm(table[...].astype(BF16), got, 1, 0).astype(BF16)
        else:
            res = mm(table[...], got.astype(F32), 1, 0, HIGHEST).astype(BF16)
        for j in range(TILES):
            out[:, 128 * j : 128 * j + 128] = res[16 * j : 16 * j + 16]

    links = [Links(ssem.at[i], rsem, MSGS * (i % 2)) for i in range(4)]
    quarter = lambda q: slice(q * QL, (q + 1) * QL)

    def gate_task(q):
        g = mm(gx[q], wg[:, quarter(q)], 1, 1)
        u = mm(gx[q], wu[:, quarter(q)], 1, 1)
        accg[...] = g if q == 0 else accg[...] + g
        accu[...] = u if q == 0 else accu[...] + u

    def act_task():
        g = accg[...]
        act_s[...] = (g * jax.nn.sigmoid(g) * accu[...]).astype(BF16)

    def out_task(q):
        oo[q] = mm(act_s[...], wd[:, quarter(q)], 1, 0).astype(BF16)

    def da_task(q):
        a = mm(gd[q], wd[:, quarter(q)], 1, 1)
        accd[...] = a if q == 0 else accd[...] + a

    def hidden_task():
        g, u, a = accg[...], accu[...], accd[...]
        s = jax.nn.sigmoid(g)
        dg_s[...] = (a * u * s * (1.0 + g * (1.0 - s))).astype(BF16)
        du_s[...] = (a * g * s).astype(BF16)

    def back_task(q):
        part = mm(dg_s[...], wg[:, quarter(q)], 1, 0) + mm(du_s[...], wu[:, quarter(q)], 1, 0)
        ob[q] = part.astype(BF16)

    def grad_task(i, q):
        left, right, out = ((dg_s, gx, gg_ref), (du_s, gx, gu_ref), (act_s, gd, gd_ref))[i]
        out[0, :, quarter(q)] = mm(left[...], right[q], 0, 0).astype(BF16)

    def task(f, *args):
        return lambda: f(*args)

    quarters = range(NX)
    exchange_out()
    exchange_in()
    assemble(0, gx)
    run_x = gather(gx, links[0], place)
    next(run_x)
    assemble(1, gd)
    run_d = gather(gd, links[1], place)
    next(run_d)
    for load in loads[4:]:
        load.wait()
    for _ in range(4):
        ring_steps(run_x, run_d)
    ring_steps(run_x)
    for q in quarters:
        gate_task(q)
    act_task()
    for q in quarters:
        out_task(q)
    run_o = scatter(oo, land_o, links[3], place)
    run_b = scatter(ob, land_b, links[2], place)
    ring_steps(run_o)
    ring_steps(run_o)
    ring_steps(run_o)
    ring_steps(run_d)
    for q in quarters:
        da_task(q)
    hidden_task()
    for q in quarters:
        back_task(q)
    ring_steps(run_b)
    ring_steps(run_b)
    ring_steps(run_b)
    tasks = [task(grad_task, i, q) for i in range(3) for q in quarters]
    for _ in range(10):
        ring_steps(run_o, run_b)
        for t in tasks[:2]:
            t()
        tasks = tasks[2:]
    ring_steps(run_o)
    return_out(0, oo)
    ring_steps(run_b)
    return_out(1, ob)
    return_in(0, qw, mixed_ref)
    return_in(1, qt, gtok_ref)

    for i, table in enumerate((gx, gd, ob, oo)):
        links[i].wait_sent(table, dzp)

    def wait_sent(ref, sem):
        pltpu.make_async_remote_copy(
            src_ref=ref, dst_ref=ref, send_sem=sem, recv_sem=arecv.at[0, 0],
            device_id=dzp, device_id_type=MESH,
        ).wait_send()

    wait_sent(msend.at[pl.ds(1, HOSTS - 1)], asend.at[0, 1])

    @pl.when(other)
    def _():
        wait_sent(msend.at[0], asend.at[0, 0])

    for which in range(2):
        wait_sent(rsend.at[which, :, pl.ds(1, NX - 1)], asend.at[1 + which, 2])
        for r in range(2):

            @pl.when(2 * own + r != h)
            def _():
                wait_sent(rsend.at[which, r, 0], asend.at[1 + which, r])


def write_out(*refs):
    parts, outs, sem = refs[:5], refs[5:10], refs[10]
    copies = [pltpu.make_async_copy(parts[i], outs[i], sem.at[i]) for i in range(5)]
    for copy in copies:
        copy.start()
    for copy in copies:
        copy.wait()


def body(tokens, cotangent, expert_ids, gate_values, w_gate, w_up, w_down):
    vmem, hbm = pl.BlockSpec(memory_space=pltpu.VMEM), pl.BlockSpec(memory_space=pl.ANY)
    shapes = [(TOK, FEAT)] * 2 + [(1, FF, D)] * 3
    landing = [
        pltpu.VMEM((2, 4, NX, ROWS, LA), BF16),
        pltpu.VMEM((2, 4, ROWS, QL - LA), BF16),
        pltpu.VMEM((3, ROWS, LA), BF16),
        pltpu.VMEM((3, ROWS, QL - LA), BF16),
        pltpu.VMEM((2, R, (QL - LA) // 2), BF16),
        pltpu.VMEM((2, R, QL - LA), BF16),
    ]
    weight, table = pltpu.VMEM((FF, D), BF16), pltpu.VMEM((NX, R, QL), BF16)
    acc, hid = pltpu.VMEM((R, FF), F32), pltpu.VMEM((R, FF), BF16)
    parts = pl.pallas_call(
        kernel,
        out_shape=[pltpu.VMEM(shape, BF16) for shape in shapes],
        in_specs=[hbm] * 7,
        out_specs=[vmem] * 5,
        scratch_shapes=[
            pltpu.VMEM((TOK, FEAT), BF16), pltpu.VMEM((TOK, FEAT), BF16),
            pltpu.VMEM((2, TOK), jnp.int32), pltpu.VMEM((2, TOK), F32),
            weight, weight, weight, table, table, table, table, acc, acc, acc, hid, hid, hid,
            pltpu.VMEM((8 * TOK, HOSTS * 32), F32), pltpu.VMEM((8 * TOK, HOSTS * 32), F32),
            pltpu.VMEM((HOSTS, 64, 128), BF16), pltpu.VMEM((2, NX, 64, 128), BF16),
            pltpu.VMEM((2, 2, NX, 32, 128), BF16), pltpu.VMEM((2, HOSTS, 32, 128), BF16),
            *landing, *landing,
            pltpu.SemaphoreType.DMA((7,)),
            pltpu.SemaphoreType.DMA((4, 2)), pltpu.SemaphoreType.DMA((2 * MSGS,)),
            pltpu.SemaphoreType.DMA((3, 3)), pltpu.SemaphoreType.DMA((3, 8)),
        ],
        compiler_params=pltpu.CompilerParams(
            collective_id=0, has_side_effects=True, vmem_limit_bytes=52 * 1024 * 1024
        ),
    )(tokens, cotangent, expert_ids.T, gate_values.T, w_gate, w_up, w_down)
    return pl.pallas_call(
        write_out,
        out_shape=[jax.ShapeDtypeStruct(shape, BF16) for shape in shapes],
        in_specs=[vmem] * 5,
        out_specs=[hbm] * 5,
        scratch_shapes=[pltpu.SemaphoreType.DMA((5,))],
        compiler_params=pltpu.CompilerParams(vmem_limit_bytes=1024 * 1024),
    )(*[pltpu.with_memory_space_constraint(part, pltpu.VMEM) for part in parts])


def solution(mesh):
    return jax.shard_map(
        body,
        mesh=mesh,
        in_specs=(
            P("dp", "hst"),
            P("dp", "hst"),
            P("dp", None),
            P("dp", None),
            P("hst", "dp", None),
            P("hst", "dp", None),
            P("hst", "dp", None),
        ),
        out_specs=(
            P("dp", "hst"),
            P("dp", "hst"),
            P("hst", "dp", None),
            P("hst", "dp", None),
            P("hst", "dp", None),
        ),
        check_vma=False,
    )
```

```python
import jax
import jax.numpy as jnp
from jax import lax
from jax.experimental import pallas as pl
from jax.experimental.pallas import tpu as pltpu
from jax.sharding import PartitionSpec as P

F32, BF16 = jnp.float32, jnp.bfloat16
HIGHEST = lax.Precision.HIGHEST
MESH = pl.DeviceIdType.MESH
NX, NZ, HOSTS, CAP, TOK = 4, 8, 8, 4, 16
ROWS = NX * CAP
R = NZ * ROWS
FEAT = 896
QL = 2 * FEAT
D = NX * QL
FF = 152
LA = 768
TILES = FEAT // 128
MSGS = 54
PLACE = {0: 0, 1: 1, 7: 2, 2: 3, 6: 4, 3: 5, 5: 6, 4: 7}
CHUNKS = ((0, 16), (16, 32), (48, 32), (80, 32), (112, 16))


def rows(k):
    return pl.ds(ROWS * PLACE[k % NZ], ROWS)


def iota(shape, dim):
    return lax.broadcasted_iota(jnp.int32, shape, dim)


def mm(a, b, ca, cb, precision=None):
    return lax.dot_general(
        a, b, (((ca,), (cb,)), ((), ())), precision=precision, preferred_element_type=F32
    )


def add(total, part):
    total[...] = (total[...].astype(F32) + part[...].astype(F32)).astype(BF16)


def add2(total, one, two):
    parts = one[...].astype(F32) + two[...].astype(F32)
    total[...] = (total[...].astype(F32) + parts).astype(BF16)


class Links:
    def __init__(self, ssem, rsem, first):
        self.ssem, self.rsem, self.next = ssem, rsem, first

    def copy(self, src, dst, dev, i, group):
        return pltpu.make_async_remote_copy(
            src_ref=src, dst_ref=dst, send_sem=self.ssem.at[group], recv_sem=self.rsem.at[i],
            device_id=dev, device_id_type=MESH,
        )

    def send(self, src, dst, land, dev, group):
        i = self.next
        self.next += 1
        self.copy(src, dst, dev, i, group).start()
        return self.copy(land, land, dev, i, group).wait_recv

    def wait_sent(self, table, dev):
        for group, ref in ((0, table.at[0, pl.ds(0, 112)]), (1, table.at[pl.ds(0, 3)])):
            self.copy(ref, ref, dev, 0, group).wait_send()


def ring_steps(*gens):
    for g in gens:
        next(g, None)


def gather(G, links, place):
    x, xp, xm, xo, dxp, dxm, dxo, dzp, dzm = place

    def straight(rs, lo, hi):
        lanes = pl.ds(lo, hi - lo)
        mine = G.at[x, rs, lanes]
        waits = [
            links.send(mine, mine, G.at[q, rs, lanes], dev, 1)
            for q, dev in ((xo, dxo), (xm, dxp), (xp, dxm))
        ]
        yield
        for wait in waits:
            wait()

    def along_x(rs, lo, hi):
        mid = (lo + hi) // 2
        a, b = pl.ds(lo, mid - lo), pl.ds(mid, hi - mid)
        full = pl.ds(lo, hi - lo)
        mine = G.at[x, rs, full]
        p = links.send(mine, mine, G.at[xm, rs, full], dxp, 1)
        m = links.send(mine, mine, G.at[xp, rs, full], dxm, 1)
        yield
        p()
        f = links.send(G.at[xm, rs, a], G.at[xm, rs, a], G.at[xo, rs, a], dxp, 1)
        m()
        g = links.send(G.at[xp, rs, b], G.at[xp, rs, b], G.at[xo, rs, b], dxm, 1)
        yield
        f()
        g()

    def along_z(q, lo, hi, group):
        mid = (lo + hi) // 2
        p = m = None
        for s in range(1, NZ // 2 + 1):
            if s > 1:
                p()
            lu = pl.ds(lo, hi - lo) if s < NZ // 2 else pl.ds(lo, mid - lo)
            ld = pl.ds(lo, hi - lo) if s < NZ // 2 else pl.ds(mid, hi - mid)
            there = G.at[q, rows(-s), lu]
            p = links.send(G.at[q, rows(1 - s), lu], there, there, dzp, group)
            if s > 1:
                m()
            there = G.at[q, rows(s), ld]
            m = links.send(G.at[q, rows(s - 1), ld], there, there, dzm, group)
            yield
        p()
        m()

    own = along_z(x, 0, QL, 0)
    a1 = straight(rows(0), 0, LA)
    b2 = [along_x(pl.ds(lo, n), LA, QL) for lo, n in CHUNKS[:-1]]
    b2.append(straight(pl.ds(*CHUNKS[-1]), LA, QL))
    a2 = [along_z(q, 0, LA, 1) for q in (xp, xm, xo)]
    ring_steps(own, a1, b2[0])
    yield
    ring_steps(a1, *a2, own, b2[1], b2[0])
    yield
    ring_steps(own, b2[2], b2[1], *a2)
    yield
    ring_steps(own, b2[3], b2[2], *a2, b2[0])
    yield
    ring_steps(own, b2[4], b2[3], *a2, b2[1])
    yield
    ring_steps(*a2, *b2)


def scatter(O, landing, links, place):
    x, xp, xm, xo, dxp, dxm, dxo, dzp, dzm = place
    za, zb, xa, xb, xb1, xb2 = landing

    def straight(rs, lo, hi, land):
        lanes = pl.ds(lo, hi - lo)
        waits = [
            links.send(O.at[q, rs, lanes], land.at[i], land.at[i], dev, 0)
            for i, (q, dev) in enumerate(((xo, dxo), (xp, dxp), (xm, dxm)))
        ]
        yield
        for wait in waits:
            wait()
        total = O.at[x, rs, lanes]
        parts = [land[i].astype(F32) for i in range(3)]
        total[...] = (total[...].astype(F32) + (parts[0] + parts[1] + parts[2])).astype(BF16)

    def along_x(rs, lo, hi):
        mid = (lo + hi) // 2
        n = mid - lo
        a, b = pl.ds(lo, n), pl.ds(mid, n)
        full = pl.ds(lo, hi - lo)
        ha, hb = xb1.at[0, rs], xb1.at[1, rs]
        wa, wb = xb2.at[0, rs], xb2.at[1, rs]
        p = links.send(O.at[xo, rs, a], ha, ha, dxp, 1)
        m = links.send(O.at[xo, rs, b], hb, hb, dxm, 1)
        yield
        p()
        add(O.at[xp, rs, a], ha)
        p = links.send(O.at[xp, rs, full], wa, wa, dxp, 1)
        m()
        add(O.at[xm, rs, b], hb)
        m = links.send(O.at[xm, rs, full], wb, wb, dxm, 1)
        yield
        p()
        m()
        add2(O.at[x, rs, full], wa, wb)

    def along_z(q, lq, lo, hi, land, group):
        mid = (lo + hi) // 2
        n = mid - lo
        a, b = pl.ds(lo, n), pl.ds(mid, n)
        full = pl.ds(lo, hi - lo)

        def at(d, s):
            ref = land.at[d, s] if lq is None else land.at[d, s, lq]
            if s:
                return ref
            return ref.at[:, pl.ds(0, n)] if lq is None else ref.at[:, :, pl.ds(0, n)]

        far = NZ // 2
        m = links.send(O.at[q, rows(far), a], at(0, 0), at(0, 0), dzm, group)
        p = links.send(O.at[q, rows(far), b], at(1, 0), at(1, 0), dzp, group)
        yield
        for s in range(1, far):
            k = far - s
            m()
            add(O.at[q, rows(-k), a if s == 1 else full], at(0, s - 1))
            m = links.send(O.at[q, rows(-k), full], at(0, s), at(0, s), dzm, group)
            p()
            add(O.at[q, rows(k), b if s == 1 else full], at(1, s - 1))
            p = links.send(O.at[q, rows(k), full], at(1, s), at(1, s), dzp, group)
            yield
        m()
        p()
        add2(O.at[q, rows(0), full], at(0, far - 1), at(1, far - 1))

    az = [along_z(pl.ds(2 * i, 2), pl.ds(2 * i, 2), 0, LA, za, 1) for i in range(2)]
    bx = [along_x(pl.ds(lo, n), LA, QL) for lo, n in CHUNKS[:-1]]
    bx.append(straight(pl.ds(*CHUNKS[-1]), LA, QL, xb))
    bz = along_z(x, None, LA, QL, zb, 0)
    ax = straight(rows(0), 0, LA, xa)
    ring_steps(az[0])
    yield
    ring_steps(az[1])
    yield
    ring_steps(bx[4], bx[3])
    yield
    ring_steps(bx[2])
    yield
    ring_steps(*az)
    yield
    ring_steps(bx[4], bz, bx[3])
    yield
    ring_steps(bx[1])
    yield
    ring_steps(*az)
    yield
    ring_steps(bx[3], bz, bx[2])
    yield
    ring_steps(bx[0])
    yield
    ring_steps(*az)
    yield
    ring_steps(bx[2], bz, bx[1])
    yield
    ring_steps(*az, ax)
    yield
    ring_steps(bx[1], bz, bx[0])
    yield
    ring_steps(bx[0], ax, bz)


def kernel(
    tok_hbm, cot_hbm, ids_hbm, gate_hbm, wg_hbm, wu_hbm, wd_hbm,
    mixed_ref, gtok_ref, gg_ref, gu_ref, gd_ref,
    tok_ref, cot_ref, ids_ref, gate_ref, wg, wu, wd, gx, gd, oo, ob, accg, accu, accd, act_s, dg_s, du_s, qt, qw,
    msend, mrecv, rsend, rrecv, *rest,
):
    land_o, land_b = rest[0:6], rest[6:12]
    wsem, ssem, rsem, asend, arecv = rest[12:]
    dp, h = lax.axis_index("dp"), lax.axis_index("hst")
    z, x = dp // NX, dp % NX
    xp, xm, xo = (x + 1) % NX, (x + NX - 1) % NX, (x + 2) % NX
    dev = lambda zz, xx, hh: (zz * NX + xx, hh)
    dxp, dxm = dev(z, xp, h), dev(z, xm, h)
    dxo = dev(z, xo, h)
    dzp, dzm = dev((z + 1) % NZ, x, h), dev((z + NZ - 1) % NZ, x, h)
    hq, hr = h // 2, h % 2
    own = (x - hq + NX) % NX
    turned = [(own + i) % NX for i in (0, 1, NX - 1, 2)]
    place = (*turned, dxp, dxm, dxo, dzp, dzm)
    other = own != hq
    owner = lambda e: dev(z, (hq + e // 2) % NX, e)
    source = lambda xx, r: dev(z, xx, 2 * own + r)

    small = ((ids_hbm, ids_ref), (gate_hbm, gate_ref), (tok_hbm, tok_ref), (cot_hbm, cot_ref))
    large = ((wg_hbm.at[0], wg), (wu_hbm.at[0], wu), (wd_hbm.at[0], wd))
    loads = [
        pltpu.make_async_copy(src, dst, wsem.at[i]) for i, (src, dst) in enumerate(small + large)
    ]
    for load in loads:
        load.start()

    barrier = pltpu.get_barrier_semaphore()

    def greet(device):
        pl.semaphore_signal(barrier, inc=1, device_id=device, device_id_type=MESH)

    turn = (hq - own + NX) % NX
    greet(dzp)
    greet(dzm)
    for k in range(1, HOSTS):
        greet(owner((h + k) % HOSTS))
    for i in range(1, NX):
        for r in range(2):
            greet(source((x + i) % NX, r))

    @pl.when(other)
    def _():
        greet(owner(h))

        @pl.when(turn != 1)
        def _():
            greet(dxp)

        @pl.when(turn != 3)
        def _():
            greet(dxm)

        @pl.when(turn != 2)
        def _():
            greet(dxo)

    for load in loads[:4]:
        load.wait()
    eye = iota((TOK, TOK), 0) == iota((TOK, TOK), 1)

    def column(ref, k):
        return jnp.sum(jnp.where(eye, ref[k : k + 1, :], 0), axis=1, keepdims=True)

    id0, id1 = column(ids_ref, 0), column(ids_ref, 1)
    gate0, gate1 = column(gate_ref, 0), column(gate_ref, 1)
    lane = iota((TOK, HOSTS * CAP), 1)
    expert, slot = lane // CAP, (lane % CAP).astype(F32)
    hit0 = (id0 == expert).astype(F32)
    hit1 = (id1 == expert).astype(F32)
    below = (iota((TOK, TOK), 0) > iota((TOK, TOK), 1)).astype(BF16)
    before = mm(below, (hit0 + hit1).astype(BF16), 1, 0)
    hit0 = jnp.where(before == slot, hit0, 0.0)
    hit1 = jnp.where(before + (id0 == expert).astype(F32) == slot, hit1, 0.0)
    wide = (HOSTS * CAP, HOSTS * 32)
    spread = (
        (iota(wide, 0) // CAP == iota(wide, 1) // 32)
        & (iota(wide, 0) % CAP == iota(wide, 1) % CAP)
    ).astype(F32)
    sel = mm(hit0 + hit1, spread, 1, 0, HIGHEST)
    wei = mm(hit0 * gate0 + hit1 * gate1, spread, 1, 0, HIGHEST)
    big = (8 * TOK, HOSTS * 32)
    tile = iota(big, 0) // TOK
    same = (tile == (iota(big, 1) // CAP) % 8) & (tile < TILES)
    qt[...] = jnp.where(same, jnp.concatenate([sel] * 8, axis=0), 0.0)
    qw[...] = jnp.where(same, jnp.concatenate([wei] * 8, axis=0), 0.0)

    def stacked(ref):
        parts = [ref[:, 128 * j : 128 * j + 128] for j in range(TILES)]
        return jnp.concatenate(parts + [jnp.zeros((TOK, 128), ref.dtype)], axis=0)

    xm_rows = mm(qt[...].astype(BF16), stacked(tok_ref), 0, 0).astype(BF16)
    msend[:, 0:32] = xm_rows.reshape(HOSTS, 32, 128)
    dm_rows = mm(qw[...], stacked(cot_ref).astype(F32), 0, 0, HIGHEST).astype(BF16)
    msend[:, 32:64] = dm_rows.reshape(HOSTS, 32, 128)

    sq = (128, 128)
    bi, mi = iota(sq, 0), iota(sq, 1)

    def matches(blk, msg):
        return (
            (blk // 16 == (msg // 4) % 8)
            & ((blk // 4) % 4 == msg // 32)
            & (blk % 4 == msg % 4)
        ).astype(F32).astype(BF16)

    into_block, into_msg = matches(bi, mi), matches(mi, bi)

    pl.semaphore_wait(barrier, 18 - 3 * ((NX - turn) // NX))

    def exchange_out():
        for k in (4, 3, 5, 2, 6, 1, 7, 0):
            e = (h + k) % HOSTS
            copy = pltpu.make_async_remote_copy(
                src_ref=msend.at[e], dst_ref=mrecv.at[hr, x],
                send_sem=asend.at[0, min(k, 1)], recv_sem=arecv.at[0, hr * NX + x],
                device_id=owner(e), device_id_type=MESH,
            )
            if k:
                copy.start()
            else:
                pl.when(other)(copy.start)

        @pl.when(jnp.logical_not(other))
        def _():
            mrecv[hr, x] = msend[h]

    def exchange_in():
        for i in range(NX):
            for r in range(2):
                xi = (x + i) % NX
                land = mrecv.at[r, xi]
                copy = pltpu.make_async_remote_copy(
                    src_ref=land, dst_ref=land,
                    send_sem=asend.at[0, 0], recv_sem=arecv.at[0, r * NX + xi],
                    device_id=source(xi, r), device_id_type=MESH,
                )
                if i:
                    copy.wait_recv()
                else:
                    pl.when(2 * own + r != h)(copy.wait_recv)

    def assemble(which, block):
        for r in range(2):
            got = mrecv[r, :, 32 * which : 32 * which + 32].reshape(128, 128)
            got = mm(into_block, got, 1, 0).astype(BF16)
            for j in range(TILES):
                lo = r * FEAT + 128 * j
                block[own, 0:ROWS, lo : lo + 128] = got[16 * j : 16 * j + 16]

    def return_out(which, block):
        for r in range(2):
            parts = [
                block[own, 0:ROWS, r * FEAT + 128 * j : r * FEAT + 128 * j + 128]
                for j in range(TILES)
            ]
            parts.append(jnp.zeros((ROWS, 128), BF16))
            got = mm(into_msg, jnp.concatenate(parts, axis=0), 1, 0).astype(BF16)
            rsend[which, r] = got.reshape(NX, 32, 128)
        for i in (2, 1, 3, 0):
            for r in range(2):
                xi = (x + i) % NX
                copy = pltpu.make_async_remote_copy(
                    src_ref=rsend.at[which, r, xi], dst_ref=rrecv.at[which, h],
                    send_sem=asend.at[1 + which, 2 if i else r], recv_sem=arecv.at[1 + which, h],
                    device_id=source(xi, r), device_id_type=MESH,
                )
                if i:
                    copy.start()
                else:
                    pl.when(2 * own + r != h)(copy.start)

        @pl.when(jnp.logical_not(other))
        def _():
            rrecv[which, h] = rsend[which, hr, x]

    def return_in(which, table, out):
        for k in range(HOSTS):
            e = (h + k) % HOSTS
            land = rrecv.at[which, e]
            copy = pltpu.make_async_remote_copy(
                src_ref=land, dst_ref=land,
                send_sem=asend.at[1 + which, 0], recv_sem=arecv.at[1 + which, e],
                device_id=owner(e), device_id_type=MESH,
            )
            if k:
                copy.wait_recv()
            else:
                pl.when(other)(copy.wait_recv)
        got = rrecv[which].reshape(HOSTS * 32, 128)
        if which:
            res = mm(table[...].astype(BF16), got, 1, 0).astype(BF16)
        else:
            res = mm(table[...], got.astype(F32), 1, 0, HIGHEST).astype(BF16)
        for j in range(TILES):
            out[:, 128 * j : 128 * j + 128] = res[16 * j : 16 * j + 16]

    links = [Links(ssem.at[i], rsem, MSGS * (i % 2)) for i in range(4)]
    quarter = lambda q: slice(q * QL, (q + 1) * QL)

    def gate_task(q):
        g = mm(gx[q], wg[:, quarter(q)], 1, 1)
        u = mm(gx[q], wu[:, quarter(q)], 1, 1)
        accg[...] = g if q == 0 else accg[...] + g
        accu[...] = u if q == 0 else accu[...] + u

    def act_task():
        g = accg[...]
        act_s[...] = (g * jax.nn.sigmoid(g) * accu[...]).astype(BF16)

    def out_task(q):
        oo[q] = mm(act_s[...], wd[:, quarter(q)], 1, 0).astype(BF16)

    def da_task(q):
        a = mm(gd[q], wd[:, quarter(q)], 1, 1)
        accd[...] = a if q == 0 else accd[...] + a

    def hidden_task():
        g, u, a = accg[...], accu[...], accd[...]
        s = jax.nn.sigmoid(g)
        dg_s[...] = (a * u * s * (1.0 + g * (1.0 - s))).astype(BF16)
        du_s[...] = (a * g * s).astype(BF16)

    def back_task(q):
        part = mm(dg_s[...], wg[:, quarter(q)], 1, 0) + mm(du_s[...], wu[:, quarter(q)], 1, 0)
        ob[q] = part.astype(BF16)

    def grad_task(i, q):
        left, right, out = ((dg_s, gx, gg_ref), (du_s, gx, gu_ref), (act_s, gd, gd_ref))[i]
        out[0, :, quarter(q)] = mm(left[...], right[q], 0, 0).astype(BF16)

    def task(f, *args):
        return lambda: f(*args)

    quarters = range(NX)
    exchange_out()
    exchange_in()
    assemble(0, gx)
    run_x = gather(gx, links[0], place)
    next(run_x)
    assemble(1, gd)
    run_d = gather(gd, links[1], place)
    next(run_d)
    for load in loads[4:]:
        load.wait()
    for _ in range(4):
        ring_steps(run_x, run_d)
    ring_steps(run_x)
    for q in quarters:
        gate_task(q)
    act_task()
    run_o = scatter(oo, land_o, links[3], place)
    run_b = scatter(ob, land_b, links[2], place)
    for half in range(2):
        out_task(2 * half)
        out_task(2 * half + 1)
        ring_steps(run_o)
    ring_steps(run_o)
    ring_steps(run_o)
    ring_steps(run_d)
    for q in quarters:
        da_task(q)
    hidden_task()
    for half in range(2):
        back_task(2 * half)
        back_task(2 * half + 1)
        ring_steps(run_b)
    ring_steps(run_b)
    ring_steps(run_b)
    tasks = [task(grad_task, i, q) for i in range(3) for q in quarters]
    for _ in range(10):
        ring_steps(run_o, run_b)
        for t in tasks[:2]:
            t()
        tasks = tasks[2:]
    ring_steps(run_o)
    return_out(0, oo)
    ring_steps(run_b)
    return_out(1, ob)
    return_in(0, qw, mixed_ref)
    return_in(1, qt, gtok_ref)

    for i, table in enumerate((gx, gd, ob, oo)):
        links[i].wait_sent(table, dzp)

    def wait_sent(ref, sem):
        pltpu.make_async_remote_copy(
            src_ref=ref, dst_ref=ref, send_sem=sem, recv_sem=arecv.at[0, 0],
            device_id=dzp, device_id_type=MESH,
        ).wait_send()

    wait_sent(msend.at[pl.ds(1, HOSTS - 1)], asend.at[0, 1])

    @pl.when(other)
    def _():
        wait_sent(msend.at[0], asend.at[0, 0])

    for which in range(2):
        wait_sent(rsend.at[which, :, pl.ds(1, NX - 1)], asend.at[1 + which, 2])
        for r in range(2):

            @pl.when(2 * own + r != h)
            def _():
                wait_sent(rsend.at[which, r, 0], asend.at[1 + which, r])


def write_out(*refs):
    parts, outs, sem = refs[:5], refs[5:10], refs[10]
    copies = []
    for i in range(2, 5):
        for q in range(NX):
            piece = (slice(None), slice(None), pl.ds(q * QL, QL))
            copies.append((parts[i].at[piece], outs[i].at[piece]))
    copies += [(parts[i], outs[i]) for i in range(2)]
    copies = [pltpu.make_async_copy(*pair, sem.at[n]) for n, pair in enumerate(copies)]
    for copy in copies:
        copy.start()
    for copy in copies:
        copy.wait()


def body(tokens, cotangent, expert_ids, gate_values, w_gate, w_up, w_down):
    vmem, hbm = pl.BlockSpec(memory_space=pltpu.VMEM), pl.BlockSpec(memory_space=pl.ANY)
    shapes = [(TOK, FEAT)] * 2 + [(1, FF, D)] * 3
    landing = [
        pltpu.VMEM((2, 4, NX, ROWS, LA), BF16),
        pltpu.VMEM((2, 4, ROWS, QL - LA), BF16),
        pltpu.VMEM((3, ROWS, LA), BF16),
        pltpu.VMEM((3, ROWS, QL - LA), BF16),
        pltpu.VMEM((2, R, (QL - LA) // 2), BF16),
        pltpu.VMEM((2, R, QL - LA), BF16),
    ]
    weight, table = pltpu.VMEM((FF, D), BF16), pltpu.VMEM((NX, R, QL), BF16)
    acc, hid = pltpu.VMEM((R, FF), F32), pltpu.VMEM((R, FF), BF16)
    parts = pl.pallas_call(
        kernel,
        out_shape=[pltpu.VMEM(shape, BF16) for shape in shapes],
        in_specs=[hbm] * 7,
        out_specs=[vmem] * 5,
        scratch_shapes=[
            pltpu.VMEM((TOK, FEAT), BF16), pltpu.VMEM((TOK, FEAT), BF16),
            pltpu.VMEM((2, TOK), jnp.int32), pltpu.VMEM((2, TOK), F32),
            weight, weight, weight, table, table, table, table, acc, acc, acc, hid, hid, hid,
            pltpu.VMEM((8 * TOK, HOSTS * 32), F32), pltpu.VMEM((8 * TOK, HOSTS * 32), F32),
            pltpu.VMEM((HOSTS, 64, 128), BF16), pltpu.VMEM((2, NX, 64, 128), BF16),
            pltpu.VMEM((2, 2, NX, 32, 128), BF16), pltpu.VMEM((2, HOSTS, 32, 128), BF16),
            *landing, *landing,
            pltpu.SemaphoreType.DMA((7,)),
            pltpu.SemaphoreType.DMA((4, 2)), pltpu.SemaphoreType.DMA((2 * MSGS,)),
            pltpu.SemaphoreType.DMA((3, 3)), pltpu.SemaphoreType.DMA((3, 8)),
        ],
        compiler_params=pltpu.CompilerParams(
            collective_id=0, has_side_effects=True, vmem_limit_bytes=52 * 1024 * 1024
        ),
    )(tokens, cotangent, expert_ids.T, gate_values.T, w_gate, w_up, w_down)
    return pl.pallas_call(
        write_out,
        out_shape=[jax.ShapeDtypeStruct(shape, BF16) for shape in shapes],
        in_specs=[vmem] * 5,
        out_specs=[hbm] * 5,
        scratch_shapes=[pltpu.SemaphoreType.DMA((3 * NX + 2,))],
        compiler_params=pltpu.CompilerParams(vmem_limit_bytes=1024 * 1024),
    )(*[pltpu.with_memory_space_constraint(part, pltpu.VMEM) for part in parts])


def solution(mesh):
    return jax.shard_map(
        body,
        mesh=mesh,
        in_specs=(
            P("dp", "hst"),
            P("dp", "hst"),
            P("dp", None),
            P("dp", None),
            P("hst", "dp", None),
            P("hst", "dp", None),
            P("hst", "dp", None),
        ),
        out_specs=(
            P("dp", "hst"),
            P("dp", "hst"),
            P("hst", "dp", None),
            P("hst", "dp", None),
            P("hst", "dp", None),
        ),
        check_vma=False,
    )
```
